128 devices in a mesh: gx: 4 (over x), gy: 4 (over z_hi, core), gz: 8 (over z_lo, y).
Axes of the slice: x: 4, y: 4, z: 4 (z_hi: 2, z_lo: 2; z = z_hi * 2 + z_lo), core: 2. Of those that a mesh axis runs over, the one named last changes fastest.
Arguments:
- right_side: float32 [3, 64, 64, 1024], P(None, 'gx', 'gy', 'gz'), may hold values from -24 to 24
- labels: int32 [64, 64, 1024], P('gx', 'gy', 'gz'), may hold values from 0 to 15
- colors: int32 [3, 64, 64, 1024], P(None, 'gx', 'gy', 'gz'), may hold values from 0 to 3
- table: float32 [16], replicated, may hold values from 0.5 to 4
Outputs:
- preconditioned: float32 [3, 64, 64, 1024], P(None, 'gx', 'gy', 'gz')
The draws below stay inside these ranges and needn't reach their ends.
All inputs are finite; a program needn't handle non-finite values.
Results may differ from the reference program's by a relative error of at most 0.00002.
Values sent between devices are 32-bit elements; how exact they have to be, the bound alone decides.
A program may use at most 64 MiB of HBM per device.

```python
import math
import jax
import jax.numpy as jnp
from jax import lax

NSWEEP = 2
NCOL = 4
NCHEB = 4
NREG = 16
NX = 64
NY = 64
NZ = 1024


def touch_ends(values, own_key, smallest, high):
    longest = values.shape.index(max(values.shape))
    spots = []
    for shift in (0, 1):
        where = [jax.random.randint(jax.random.fold_in(own_key, axis), (), 0, length) for axis, length in enumerate(values.shape)]
        where[longest] = (where[longest] + shift) % values.shape[longest]
        spots.append(tuple(where))
    return values.at[spots[0]].set(smallest).at[spots[1]].set(high)


def level_of(own_key, dims, cuts, least, top_value):
    def one(dim, shards_of):
        heights = jax.random.uniform(jax.random.fold_in(jax.random.fold_in(own_key, 6), dim), (shards_of,), jnp.float32, least / len(cuts), top_value / len(cuts))
        return jnp.repeat(jnp.exp(heights), dims[dim] // shards_of).reshape((-1,) + (1,) * (len(dims) - dim - 1))

    level = one(*cuts[0])
    for cut in cuts[1:]:
        level = level * one(*cut)
    return level


def scatter_about(stream_key, shape, scale, bound, cuts=(), dtype=jnp.bfloat16):
    values = scale * jax.random.normal(stream_key, shape, jnp.float32)
    if cuts:
        values = values * level_of(stream_key, shape, cuts, -0.22, 0.18)
    return jnp.clip(values, -bound, bound).astype(dtype)


def setup_inputs(seed: int = 0) -> dict:
    key_list = jax.random.split(jax.random.key(seed), 5)
    return {
        "right_side": scatter_about(key_list[0], (3, NX, NY, NZ), 4.0, 24.0, ((1, 4), (2, 4), (3, 8)), jnp.float32),
        "labels": touch_ends(jax.random.randint(key_list[1], (NX, NY, NZ), 0, NREG), jax.random.fold_in(key_list[1], 1), 0, NREG - 1).astype(jnp.int32),
        "colors": touch_ends(jax.random.randint(key_list[2], (3, NX, NY, NZ), 0, NCOL), jax.random.fold_in(key_list[2], 1), 0, NCOL - 1).astype(jnp.int32),
        "table": jnp.clip(jnp.exp(jax.random.uniform(key_list[3], (NREG,), jnp.float32, math.log(0.5), math.log(4.0))), 0.5, 4.0),
    }


def unit_step(direction):
    return tuple(1 if position == direction else 0 for position in range(3))


def lower_step(direction):
    return tuple(1 - element for element in unit_step(direction))


def upper_step(direction):
    return tuple(1 + element for element in unit_step(direction))


def window(values, corner_at, extent):
    leading = values.ndim - 3
    begin_at = (0,) * leading + tuple(corner_at)
    finish = tuple(values.shape[:leading]) + tuple(offset + length for offset, length in zip(corner_at, extent))
    return lax.slice(values, begin_at, finish)


def shrink(values, amount):
    return tuple(number - amount for number in values.shape[-3:])


def pad_cells(values):
    return jnp.pad(values, ((0, 0),) * (values.ndim - 3) + ((1, 1),) * 3)


def face_curl(padded):
    extent = shrink(padded, 1)
    anchor = (0, 0, 0)
    face_list = []
    for normal in range(3):
        second = (normal + 1) % 3
        third_axis = (normal + 2) % 3
        face_list.append(window(padded[second], anchor, extent) - window(padded[second], unit_step(third_axis), extent)
                         + window(padded[third_axis], unit_step(second), extent) - window(padded[third_axis], anchor, extent))
    return jnp.stack(face_list)


def curl_back(faces_in):
    extent = shrink(faces_in, 1)
    centre = (1, 1, 1)
    result = []
    for edge_axis in range(3):
        before = (edge_axis + 2) % 3
        next_axis = (edge_axis + 1) % 3
        result.append(window(faces_in[before], centre, extent) - window(faces_in[before], lower_step(next_axis), extent)
                      - window(faces_in[next_axis], centre, extent) + window(faces_in[next_axis], lower_step(before), extent))
    return jnp.stack(result)


def edge_apply(padded, conduct, keep_mask):
    faces_in = face_curl(padded) * keep_mask
    inner = window(padded, (1, 1, 1), shrink(padded, 2))
    return curl_back(faces_in) + conduct * inner


def node_apply(field_ext, cond_ext, mass_weight):
    wide_extent = shrink(field_ext, 1)
    narrow_extent = shrink(field_ext, 2)
    anchor = (0, 0, 0)
    coefficient = window(cond_ext, anchor, wide_extent)
    centre_values = window(field_ext, anchor, wide_extent)
    summed = mass_weight * window(cond_ext, (1, 1, 1), narrow_extent) * window(field_ext, (1, 1, 1), narrow_extent)
    for direction in range(3):
        edge_flux = coefficient * (window(field_ext, unit_step(direction), wide_extent) - centre_values)
        summed = summed + window(edge_flux, lower_step(direction), narrow_extent) - window(edge_flux, (1, 1, 1), narrow_extent)
    return summed


def nodal_rhs(padded):
    narrow_extent = shrink(padded, 2)
    centre = (1, 1, 1)
    pieces = []
    scalar_part = None
    for direction in range(3):
        own_values = window(padded[direction], centre, narrow_extent)
        below_values = window(padded[direction], lower_step(direction), narrow_extent)
        difference = below_values - own_values
        scalar_part = difference if direction == 0 else scalar_part + difference
        pieces.append(0.5 * (own_values + below_values))
    return jnp.stack([scalar_part] + pieces)


def chebyshev(rhs_fields, apply_fn, table):
    upper = 13.0 * jnp.max(table)
    lower = upper / 30.0
    centre_value = 0.5 * (upper + lower)
    half_width = 0.5 * (upper - lower)
    ratio = centre_value / half_width
    damping = 1.0 / ratio
    solved = jnp.zeros_like(rhs_fields)
    residue = rhs_fields
    step_dir = rhs_fields / centre_value
    for degree in range(NCHEB):
        solved = solved + step_dir
        if degree + 1 < NCHEB:
            residue = residue - apply_fn(step_dir)
            damping_next = 1.0 / (2.0 * ratio - damping)
            step_dir = damping_next * damping * step_dir + (2.0 * damping_next / half_width) * residue
            damping = damping_next
    return solved


def correction(field_ext):
    narrow_extent = shrink(field_ext, 2)
    centre = (1, 1, 1)
    pieces = []
    for direction in range(3):
        gradient = window(field_ext[0], upper_step(direction), narrow_extent) - window(field_ext[0], centre, narrow_extent)
        averaged = 0.5 * (window(field_ext[1 + direction], centre, narrow_extent) + window(field_ext[1 + direction], upper_step(direction), narrow_extent))
        pieces.append(gradient + averaged)
    return jnp.stack(pieces)


def reference(right_side, labels, colors, table):
    conduct = table[labels]
    diagonal = 16.0 + conduct
    extent_plus = tuple(number + 1 for number in labels.shape)
    keep_mask = jnp.ones(extent_plus, jnp.float32)
    for position in range(3):
        counter = lax.broadcasted_iota(jnp.int32, extent_plus, position)
        keep_mask = keep_mask * jnp.where(counter > 0, 1.0, 0.0).astype(jnp.float32)
    iterate = jnp.zeros_like(right_side)
    for sweep_index in range(NSWEEP):
        for colour in range(NCOL):
            residual = right_side - edge_apply(pad_cells(iterate), conduct, keep_mask)
            iterate = iterate + jnp.where(colors == colour, residual / diagonal, 0.0)
    cond_ext = pad_cells(conduct)
    rhs_fields = nodal_rhs(pad_cells(right_side))
    mass_weight = jnp.array([0.0, 1.0, 1.0, 1.0], jnp.float32).reshape(4, 1, 1, 1)

    def apply_nodal(fields):
        return node_apply(pad_cells(fields), cond_ext, mass_weight)

    solved = chebyshev(rhs_fields, apply_nodal, table)
    return iterate + correction(pad_cells(solved))
```

```python
import functools
import itertools

import jax
import jax.numpy as jnp
from jax import lax
from jax.experimental import pallas as pl
from jax.experimental.pallas import tpu as pltpu
from jax.sharding import PartitionSpec as P

NSWEEP = 2
NCOL = 4
NCHEB = 4
AXES = ("gx", "gy", "gz")

H = 4
N = 16
B = N + 2 * H
LANES = 128
OWN = slice(H, H + N)
DIRS = [d for d in itertools.product((-1, 0, 1), repeat=3) if d != (0, 0, 0)]


def roll(values, shift, axis):
    return pltpu.roll(values, shift, axis)


def down_lane(values):
    return roll(values, 1, 1)


def up_lane(values):
    return roll(values, LANES - 1, 1)


def down_row(values):
    return roll(values, 1, 0)


def up_row(values):
    return roll(values, B - 1, 0)


def group_of(xp):
    ring = lax.rem(xp + (B - H), B)
    return ring // 8, lax.rem(ring, 8)


def select_table(labels, table):
    level = [table[i] for i in range(16)]
    for bit in range(4):
        odd = (labels & (1 << bit)) != 0
        level = [jnp.where(odd, level[i + 1], level[i]) for i in range(0, len(level), 2)]
    return level[0]


def kernel(
    sizes,
    r_hbm, lab_hbm, col_hbm, tab,
    out,
    r_in, lab_in, col_in,
    W, QM, QR, PW, INV, PINV, PMASK, PKEEP,
    E, PE, E2, PE2, QME, QRE, U,
    NR, ND, NY, PR, PD, PY, UD,
    in_sem, ssem, rsem,
):
    here = [lax.axis_index(a) for a in AXES]

    def neighbour(d):
        return tuple(lax.rem(here[i] + (d[i] + sizes[i]), sizes[i]) for i in range(3))

    barrier = pltpu.get_barrier_semaphore()
    for d in DIRS:
        pl.semaphore_signal(barrier, inc=1, device_id=neighbour(d), device_id_type=pl.DeviceIdType.MESH)
    loads = [
        pltpu.make_async_copy(src, dst, in_sem.at[i])
        for i, (src, dst) in enumerate(((lab_hbm, lab_in), (r_hbm, r_in), (col_hbm, col_in)))
    ]
    for load in loads:
        load.start()

    first = [jnp.where(here[i] > 0, 1.0, 0.0).astype(jnp.float32) for i in range(3)]
    last = [jnp.where(here[i] < sizes[i] - 1, 1.0, 0.0).astype(jnp.float32) for i in range(3)]
    lane = lax.broadcasted_iota(jnp.int32, (B, LANES), 1)
    row = lax.broadcasted_iota(jnp.int32, (B, LANES), 0)
    spot = lane % 16
    low_rows = jnp.where(row < H, first[1], 1.0)
    row_mask = low_rows * jnp.where(row >= H + N, last[1], 1.0)
    low_ends = jnp.where((spot >= 8) & (spot < 12), first[2], 1.0) * low_rows
    ends = jnp.where((spot >= 4) & (spot < 8), last[2], 1.0) * low_ends * jnp.where(
        row >= H + N, last[1], 1.0
    )
    before = jnp.where(lane >= 64, first[0], 1.0)
    after = jnp.where(lane < 64, last[0], 1.0)
    for t in range(3):
        PKEEP[t] = low_ends * before if t == 2 else low_ends
        PMASK[t] = ends * before * after if t == 2 else ends

    def x_low(xp):
        return jnp.where(xp >= H, 1.0, first[0])

    def x_mask(xp):
        return x_low(xp) * jnp.where(xp < H + N, 1.0, last[0])

    for load in loads:
        load.wait()

    @pl.loop(0, N)
    def _(x):
        W[3, x + H, OWN] = select_table(lab_in[x], tab)
        for c in range(3):
            W[c, x + H, OWN] = r_in[c, x]
            W[4 + c, x + H, OWN] = col_in[c, x].astype(jnp.float32) + 1.0

    def pack_own(src, dst, fields):
        narrow = lax.broadcasted_iota(jnp.int32, (N, LANES), 1) // 16

        @pl.loop(0, fields)
        def _(f):
            for t in range(2):
                total = None
                for g in range(8):
                    piece = roll(src[f, H + 8 * t + g, OWN], 16 * g + 4, 1)
                    total = piece if g == 0 else jnp.where(narrow == g, piece, total)
                dst[f, t, OWN] = total

    pack_own(W, QM, 7)
    pl.semaphore_wait(barrier, len(DIRS))

    def span(d, side):
        if d == 0:
            return slice(H, H + N)
        low = (d > 0) == (side == "dst")
        if side == "dst":
            return slice(0, H) if low else slice(H + N, B)
        return slice(H, 2 * H) if d < 0 else slice(N, N + H)

    def exchange(phase, main, packed, received):
        copies = []
        for i, d in enumerate(DIRS):
            rows_src, rows_dst = span(d[1], "src"), span(d[1], "dst")
            if d[2] == 0:
                src = main.at[:, span(d[0], "src"), rows_src]
                dst = main.at[:, span(d[0], "dst"), rows_dst]
            else:
                slot_src = {0: slice(0, 2), 1: slice(1, 2), -1: slice(0, 1)}[d[0]]
                slot_dst = {0: slice(0, 2), 1: slice(3, 4), -1: slice(2, 3)}[d[0]]
                src = packed.at[:, slot_src, rows_src]
                dst = received.at[1 if d[2] > 0 else 0, :, slot_dst, rows_dst]
            copies.append(
                pltpu.make_async_remote_copy(
                    src_ref=src,
                    dst_ref=dst,
                    send_sem=ssem.at[phase, i],
                    recv_sem=rsem.at[phase, i],
                    device_id=neighbour(d),
                    device_id_type=pl.DeviceIdType.MESH,
                )
            )
        order = sorted(range(len(DIRS)), key=lambda i: (-abs(DIRS[i][0]), sum(map(abs, DIRS[i]))))
        for i in order:
            copies[i].start()
        return copies

    def assemble(src, received, dst, fields):
        @pl.loop(0, fields)
        def _(f):
            for t in range(3):
                own = None
                for g in range(8):
                    x = (8 * t + g + H) % B
                    piece = roll(src[f, x], 16 * g + 4, 1)
                    own = piece if g == 0 else jnp.where(lane // 16 == g, piece, own)
                if t < 2:
                    high, low = received[0, f, t], received[1, f, t]
                else:
                    high = jnp.where(lane < 64, received[0, f, 2], received[0, f, 3])
                    low = jnp.where(lane < 64, received[1, f, 2], received[1, f, 3])
                upper = jnp.where(spot < 4, own, high)
                lower = roll(jnp.where(spot < 4, low, own), 8, 1)
                dst[f, t] = jnp.where(PMASK[t] > 0.0, jnp.where(spot < 8, upper, lower), 0.0)

    copies = exchange(0, W, QM, QR)
    for copy in copies:
        copy.wait()

    @pl.loop(0, B)
    def _(xp):
        inside = (row_mask * x_mask(xp)) > 0.0
        for f in range(7):
            W[f, xp] = jnp.where(inside, W[f, xp], 0.0)
        inverse = 1.0 / (16.0 + W[3, xp])
        INV[xp] = inverse
        for c in range(3):
            E[c, xp] = jnp.where(W[4 + c, xp] == 1.0, W[c, xp] * inverse, 0.0)

    assemble(W, QR, PW, 7)
    for t in range(3):
        PINV[t] = 1.0 / (16.0 + PW[3, t])
        for c in range(3):
            PE[c, t] = jnp.where(PW[4 + c, t] == 1.0, PW[c, t] * PINV[t], 0.0)

    def next_plane(tiles):
        moved = [roll(v, LANES - 16, 1) for v in tiles]
        return [jnp.where(lane < LANES - 16, moved[t], moved[(t + 1) % 3]) for t in range(3)]

    def previous_plane(tiles):
        moved = [roll(v, 16, 1) for v in tiles]
        return [jnp.where(lane >= 16, moved[t], moved[(t + 2) % 3]) for t in range(3)]

    def packed_turn(colour, edges):
        ex, ey, ez = ([edges[c, t] for t in range(3)] for c in range(3))
        eyx, ezx = next_plane(ey), next_plane(ez)
        fx, fy, fz = [], [], []
        for t in range(3):
            keep = PKEEP[t]
            fx.append((ey[t] - up_lane(ey[t]) + up_row(ez[t]) - ez[t]) * keep)
            fy.append((ez[t] - ezx[t] + up_lane(ex[t]) - ex[t]) * keep)
            fz.append((ex[t] - up_row(ex[t]) + eyx[t] - ey[t]) * keep)
        fyp, fzp = previous_plane(fy), previous_plane(fz)
        for t in range(3):
            U[0, t] = jnp.where(spot == 4, ex[t], roll(fy[t], LANES - 6, 1))
            U[1, t] = jnp.where(spot == 4, ey[t], roll(fx[t], LANES - 6, 1))
            back = (
                fz[t] - down_row(fz[t]) - fy[t] + down_lane(fy[t]),
                fx[t] - down_lane(fx[t]) - fz[t] + fzp[t],
                fy[t] - fyp[t] - fx[t] + down_row(fx[t]),
            )
            for c, old in enumerate((ex[t], ey[t], ez[t])):
                residual = PW[c, t] - back[c] - PW[3, t] * old
                edges[c, t] = old + jnp.where(PW[4 + c, t] == colour + 1.0, residual * PINV[t], 0.0)

    def turn(colour, edges, packed, reach, target=None):
        packed_turn(colour, packed)

        def faces(xp):
            t, g = group_of(xp)
            shift = lax.rem(251 - 16 * g, LANES)
            end_x, end_y = roll(U[0, t], shift, 1), roll(U[1, t], shift, 1)
            ex, ey, ez = (edges[c, xp] for c in range(3))
            ex_z = jnp.where(lane == LANES - 1, end_x, up_lane(ex))
            ey_z = jnp.where(lane == LANES - 1, end_y, up_lane(ey))
            keep = low_rows * x_low(xp)
            fx = (ey - ey_z + up_row(ez) - ez) * keep
            fy = (ez - edges[2, xp + 1] + ex_z - ex) * keep
            fz = (ex - up_row(ex) + edges[1, xp + 1] - ey) * keep
            return fx, fy, fz, end_x, end_y, (ex, ey, ez)

        def body(xp, carry):
            fyp, fzp = carry
            fx, fy, fz, end_x, end_y, old = faces(xp)
            fx_z = jnp.where(lane == 0, end_y, down_lane(fx))
            fy_z = jnp.where(lane == 0, end_x, down_lane(fy))
            back = (
                fz - down_row(fz) - fy + fy_z,
                fx - fx_z - fz + fzp,
                fy - fyp - fx + down_row(fx),
            )
            sigma, inverse = W[3, xp], INV[xp]
            for c in range(3):
                residual = W[c, xp] - back[c] - sigma * old[c]
                value = old[c] + jnp.where(W[4 + c, xp] == colour + 1.0, residual * inverse, 0.0)
                if target is None:
                    edges[c, xp] = value
                else:
                    target[c, xp, OWN] = value[OWN]
            return fy, fz

        start = faces(H - reach - 1)
        lax.fori_loop(H - reach, H + N + reach, body, (start[1], start[2]))

    turn(1, E, PE, 2)
    turn(2, E, PE, 1)
    turn(3, E, PE, 0, target=E2)

    pack_own(E2, QME, 3)
    copies = exchange(1, E2, QME, QRE)

    top = tab[0]
    for i in range(1, 16):
        top = jnp.maximum(top, tab[i])
    upper = jnp.full((B, LANES), 13.0 * top, jnp.float32)
    ratio = 31.0 / 29.0
    per_centre = (60.0 / 31.0) / upper
    per_half = (60.0 / 29.0) / upper

    @pl.loop(1, B)
    def _(xp):
        t, g = group_of(xp)
        end = roll(PW[2, t], lax.rem(245 - 16 * g, LANES), 1)
        inside = (row_mask * x_mask(xp)) > 0.0
        own = [W[c, xp] for c in range(3)]
        below = [W[0, xp - 1], down_row(own[1]), jnp.where(lane == 0, end, down_lane(own[2]))]
        values = [(below[0] - own[0]) + (below[1] - own[1]) + (below[2] - own[2])]
        values += [0.5 * (own[c] + below[c]) for c in range(3)]
        for f in range(4):
            value = jnp.where(inside, values[f], 0.0)
            NR[f, xp] = value
            value = value * per_centre
            ND[f, xp] = value
            NY[f, xp] = value

    own = [[PW[c, t] for t in range(3)] for c in range(3)]
    below = [
        previous_plane(own[0]),
        [down_row(v) for v in own[1]],
        [down_lane(v) for v in own[2]],
    ]
    for t in range(3):
        values = [sum((below[c][t] - own[c][t]) for c in range(3))]
        values += [0.5 * (own[c][t] + below[c][t]) for c in range(3)]
        for f in range(4):
            value = jnp.where(PMASK[t] > 0.0, values[f], 0.0)
            PR[f, t] = value
            value = value * per_centre
            PD[f, t] = value
            PY[f, t] = value

    rho = 1.0 / ratio
    for n in range(1, NCHEB):
        rho_next = 1.0 / (2.0 * ratio - rho)
        keep_part = rho_next * rho
        new_part = (2.0 * rho_next) * per_half
        rho = rho_next

        @pl.loop(0, 4)
        def _(f, keep_part=keep_part, new_part=new_part):
            mass = jnp.where(f > 0, 1.0, 0.0)
            d = [PD[f, t] for t in range(3)]
            dx = next_plane(d)
            sigma = [PW[3, t] for t in range(3)]
            wx = [sigma[t] * (dx[t] - d[t]) for t in range(3)]
            wxp = previous_plane(wx)
            for t in range(3):
                wy = sigma[t] * (up_row(d[t]) - d[t])
                wz = sigma[t] * (up_lane(d[t]) - d[t])
                UD[f, t] = jnp.where(spot == 4, d[t], roll(wz, LANES - 6, 1))
                applied = (
                    mass * sigma[t] * d[t]
                    + (wxp[t] - wx[t]) + (down_row(wy) - wy) + (down_lane(wz) - wz)
                )
                res = PR[f, t] - applied
                PR[f, t] = res
                new = jnp.where(PMASK[t] > 0.0, keep_part * d[t] + new_part * res, 0.0)
                PD[f, t] = new
                PY[f, t] = PY[f, t] + new

        def node_body(xp, carry, keep_part=keep_part, new_part=new_part):
            t, g = group_of(xp)
            shift = lax.rem(251 - 16 * g, LANES)
            sigma = W[3, xp]
            inside = (row_mask * x_mask(xp)) > 0.0
            fluxes = []
            for f in range(4):
                end = roll(UD[f, t], shift, 1)
                d = ND[f, xp]
                wx = sigma * (ND[f, xp + 1] - d)
                wy = sigma * (up_row(d) - d)
                wz = sigma * (jnp.where(lane == LANES - 1, end, up_lane(d)) - d)
                applied = (
                    (carry[f] - wx) + (down_row(wy) - wy)
                    + (jnp.where(lane == 0, end, down_lane(wz)) - wz)
                )
                if f > 0:
                    applied = applied + sigma * d
                res = NR[f, xp] - applied
                NR[f, xp] = res
                new = jnp.where(inside, keep_part * d + new_part * res, 0.0)
                ND[f, xp] = new
                NY[f, xp] = NY[f, xp] + new
                fluxes.append(wx)
            return tuple(fluxes)

        low, high = n + 1, B - n
        begin = tuple(W[3, low - 1] * (ND[f, low] - ND[f, low - 1]) for f in range(4))
        lax.fori_loop(low, high, node_body, begin)

    @pl.loop(0, N)
    def _(x):
        xp = x + H
        t, g = group_of(xp)
        shift = lax.rem(251 - 16 * g, LANES)
        potential = NY[0, xp]
        last_lane = lane == LANES - 1
        pieces = (
            (NY[0, xp + 1], NY[1, xp], NY[1, xp + 1]),
            (up_row(potential), NY[2, xp], up_row(NY[2, xp])),
            (
                jnp.where(last_lane, roll(PY[0, t], shift, 1), up_lane(potential)),
                NY[3, xp],
                jnp.where(last_lane, roll(PY[3, t], shift, 1), up_lane(NY[3, xp])),
            ),
        )
        for c, (above, own_part, next_part) in enumerate(pieces):
            out[c, x] = ((above - potential) + 0.5 * (own_part + next_part))[OWN]

    for copy in copies:
        copy.wait()

    @pl.loop(0, B)
    def _(xp):
        inside = (row_mask * x_mask(xp)) > 0.0
        for c in range(3):
            E2[c, xp] = jnp.where(inside, E2[c, xp], 0.0)

    assemble(E2, QRE, PE2, 3)
    for colour in range(4):
        turn(colour, E2, PE2, 3 - colour)

    @pl.loop(0, N)
    def _(x):
        for c in range(3):
            out[c, x] = out[c, x] + E2[c, x + H, OWN]


def solution(mesh):
    sizes = tuple(mesh.shape[a] for a in AXES)

    def on_device(right_side, labels, colors, table):
        f32 = jnp.float32
        plain = lambda n: pltpu.VMEM((n, B, B, LANES), f32)
        packed = lambda n: pltpu.VMEM((n, 3, B, LANES), f32)
        any_spec = pl.BlockSpec(memory_space=pl.ANY)
        return pl.pallas_call(
            functools.partial(kernel, sizes),
            out_shape=jax.ShapeDtypeStruct(right_side.shape, f32),
            in_specs=[any_spec, any_spec, any_spec, pl.BlockSpec(memory_space=pltpu.SMEM)],
            out_specs=pl.BlockSpec(memory_space=pltpu.VMEM),
            scratch_shapes=[
                pltpu.VMEM((3, N, N, LANES), f32),
                pltpu.VMEM((N, N, LANES), jnp.int32),
                pltpu.VMEM((3, N, N, LANES), jnp.int32),
                plain(7),
                pltpu.VMEM((7, 2, B, LANES), f32),
                pltpu.VMEM((2, 7, 4, B, LANES), f32),
                packed(7),
                pltpu.VMEM((B, B, LANES), f32),
                pltpu.VMEM((3, B, LANES), f32),
                pltpu.VMEM((3, B, LANES), f32),
                pltpu.VMEM((3, B, LANES), f32),
                plain(3),
                packed(3),
                plain(3),
                packed(3),
                pltpu.VMEM((3, 2, B, LANES), f32),
                pltpu.VMEM((2, 3, 4, B, LANES), f32),
                packed(2),
                plain(4),
                plain(4),
                plain(4),
                packed(4),
                packed(4),
                packed(4),
                packed(4),
                pltpu.SemaphoreType.DMA((3,)),
                pltpu.SemaphoreType.DMA((2, len(DIRS))),
                pltpu.SemaphoreType.DMA((2, len(DIRS))),
            ],
            compiler_params=pltpu.CompilerParams(
                collective_id=0, has_side_effects=True, vmem_limit_bytes=40 * 1024 * 1024
            ),
            cost_estimate=pl.CostEstimate(flops=10**8, bytes_accessed=2 * 10**6, transcendentals=0),
        )(right_side, labels, colors, table)

    in_specs = (P(None, "gx", "gy", "gz"), P("gx", "gy", "gz"), P(None, "gx", "gy", "gz"), P())
    return jax.shard_map(
        on_device, mesh=mesh, in_specs=in_specs, out_specs=P(None, "gx", "gy", "gz"), check_vma=False
    )
```

```python
import functools
import itertools

import jax
import jax.numpy as jnp
from jax import lax
from jax.experimental import pallas as pl
from jax.experimental.pallas import tpu as pltpu
from jax.sharding import PartitionSpec as P

NSWEEP = 2
NCOL = 4
NCHEB = 4
AXES = ("gx", "gy", "gz")

H = 4
N = 16
B = N + 2 * H
LANES = 128
BATCH = 5
NBATCH = 7
OWN = slice(H, H + N)
DIRS = [d for d in itertools.product((-1, 0, 1), repeat=3) if d != (0, 0, 0)]


def roll(values, shift, axis):
    return pltpu.roll(values, shift, axis)


def down_lane(values):
    return roll(values, 1, 1)


def up_lane(values):
    return roll(values, LANES - 1, 1)


def down_row(values):
    return roll(values, 1, 0)


def up_row(values):
    return roll(values, B - 1, 0)


def group_of(xp):
    ring = (xp + (B - H)) % B if isinstance(xp, int) else jnp.where(xp >= H, xp - H, xp + (B - H))
    return ring >> 3, ring & 7


def select_table(labels, table):
    level = [table[i] for i in range(16)]
    for bit in range(4):
        odd = (labels & (1 << bit)) != 0
        level = [jnp.where(odd, level[i + 1], level[i]) for i in range(0, len(level), 2)]
    return level[0]


def kernel(
    sizes,
    r_hbm, lab_hbm, col_hbm, tab,
    out,
    r_in, lab_in, col_in,
    W, QM, QR, PW, INV, PINV, PMASK, PKEEP,
    E, PE, E2, PE2, QME, QRE, U,
    NR, ND, NY, PR, PD, PY, UD,
    in_sem, ssem, rsem,
):
    here = [lax.axis_index(a) for a in AXES]
    places = [
        {
            0: here[i],
            1: jnp.where(here[i] == sizes[i] - 1, 0, here[i] + 1),
            -1: jnp.where(here[i] == 0, sizes[i] - 1, here[i] - 1),
        }
        for i in range(3)
    ]

    def neighbour(d):
        return tuple(places[i][d[i]] for i in range(3))

    barrier = pltpu.get_barrier_semaphore()
    for d in DIRS:
        pl.semaphore_signal(barrier, inc=1, device_id=neighbour(d), device_id_type=pl.DeviceIdType.MESH)
    loads = [
        pltpu.make_async_copy(src, dst, in_sem.at[i])
        for i, (src, dst) in enumerate(((lab_hbm, lab_in), (r_hbm, r_in), (col_hbm, col_in)))
    ]
    for load in loads:
        load.start()

    first = [jnp.where(here[i] > 0, 1.0, 0.0).astype(jnp.float32) for i in range(3)]
    last = [jnp.where(here[i] < sizes[i] - 1, 1.0, 0.0).astype(jnp.float32) for i in range(3)]
    lane = lax.broadcasted_iota(jnp.int32, (B, LANES), 1)
    row = lax.broadcasted_iota(jnp.int32, (B, LANES), 0)
    spot = lane % 16
    low_rows = jnp.where(row < H, first[1], 1.0)
    row_mask = low_rows * jnp.where(row >= H + N, last[1], 1.0)
    low_ends = jnp.where((spot >= 8) & (spot < 12), first[2], 1.0) * low_rows
    ends = jnp.where((spot >= 4) & (spot < 8), last[2], 1.0) * low_ends * jnp.where(
        row >= H + N, last[1], 1.0
    )
    before = jnp.where(lane >= 64, first[0], 1.0)
    after = jnp.where(lane < 64, last[0], 1.0)
    for t in range(3):
        PKEEP[t] = low_ends * before if t == 2 else low_ends
        PMASK[t] = ends * before * after if t == 2 else ends

    def x_low(xp):
        if isinstance(xp, int):
            return first[0] if xp < H else 1.0
        return jnp.where(xp >= H, 1.0, first[0])

    def x_mask(xp):
        if isinstance(xp, int):
            return last[0] if xp >= H + N else x_low(xp)
        return x_low(xp) * jnp.where(xp < H + N, 1.0, last[0])

    for load in loads:
        load.wait()

    @pl.loop(0, N)
    def _(x):
        W[3, x + H, OWN] = select_table(lab_in[x], tab)
        for c in range(3):
            W[c, x + H, OWN] = r_in[c, x]
            W[4 + c, x + H, OWN] = col_in[c, x].astype(jnp.float32) + 1.0

    def pack_own(src, dst, fields):
        narrow = lax.broadcasted_iota(jnp.int32, (N, LANES), 1) // 16

        @pl.loop(0, fields)
        def _(f):
            for t in range(2):
                total = None
                for g in range(8):
                    piece = roll(src[f, H + 8 * t + g, OWN], 16 * g + 4, 1)
                    total = piece if g == 0 else jnp.where(narrow == g, piece, total)
                dst[f, t, OWN] = total

    pack_own(W, QM, 7)
    pl.semaphore_wait(barrier, len(DIRS))

    def span(d, side):
        if d == 0:
            return slice(H, H + N)
        low = (d > 0) == (side == "dst")
        if side == "dst":
            return slice(0, H) if low else slice(H + N, B)
        return slice(H, 2 * H) if d < 0 else slice(N, N + H)

    def exchange(phase, main, packed, received):
        copies = []
        for i, d in enumerate(DIRS):
            rows_src, rows_dst = span(d[1], "src"), span(d[1], "dst")
            if d[2] == 0:
                src = main.at[:, span(d[0], "src"), rows_src]
                dst = main.at[:, span(d[0], "dst"), rows_dst]
            else:
                slot_src = {0: slice(0, 2), 1: slice(1, 2), -1: slice(0, 1)}[d[0]]
                slot_dst = {0: slice(0, 2), 1: slice(3, 4), -1: slice(2, 3)}[d[0]]
                src = packed.at[:, slot_src, rows_src]
                dst = received.at[1 if d[2] > 0 else 0, :, slot_dst, rows_dst]
            copies.append(
                pltpu.make_async_remote_copy(
                    src_ref=src,
                    dst_ref=dst,
                    send_sem=ssem.at[phase, i],
                    recv_sem=rsem.at[phase, i],
                    device_id=neighbour(d),
                    device_id_type=pl.DeviceIdType.MESH,
                )
            )
        order = sorted(range(len(DIRS)), key=lambda i: (-abs(DIRS[i][0]), sum(map(abs, DIRS[i]))))
        for i in order:
            copies[i].start()
        return copies

    def assemble(src, received, dst, fields):
        @pl.loop(0, fields)
        def _(f):
            for t in range(3):
                own = None
                for g in range(8):
                    x = (8 * t + g + H) % B
                    piece = roll(src[f, x], 16 * g + 4, 1)
                    own = piece if g == 0 else jnp.where(lane // 16 == g, piece, own)
                if t < 2:
                    high, low = received[0, f, t], received[1, f, t]
                else:
                    high = jnp.where(lane < 64, received[0, f, 2], received[0, f, 3])
                    low = jnp.where(lane < 64, received[1, f, 2], received[1, f, 3])
                upper = jnp.where(spot < 4, own, high)
                lower = roll(jnp.where(spot < 4, low, own), 8, 1)
                dst[f, t] = jnp.where(PMASK[t] > 0.0, jnp.where(spot < 8, upper, lower), 0.0)

    copies = exchange(0, W, QM, QR)
    for copy in copies:
        copy.wait()

    @pl.loop(0, B)
    def _(xp):
        inside = (row_mask * x_mask(xp)) > 0.0
        for f in range(7):
            W[f, xp] = jnp.where(inside, W[f, xp], 0.0)
        inverse = 1.0 / (16.0 + W[3, xp])
        INV[xp] = inverse
        for c in range(3):
            E[c, xp] = jnp.where(W[4 + c, xp] == 1.0, W[c, xp] * inverse, 0.0)

    assemble(W, QR, PW, 7)
    for t in range(3):
        PINV[t] = 1.0 / (16.0 + PW[3, t])
        for c in range(3):
            PE[c, t] = jnp.where(PW[4 + c, t] == 1.0, PW[c, t] * PINV[t], 0.0)

    def next_plane(tiles):
        moved = [roll(v, LANES - 16, 1) for v in tiles]
        return [jnp.where(lane < LANES - 16, moved[t], moved[(t + 1) % 3]) for t in range(3)]

    def previous_plane(tiles):
        moved = [roll(v, 16, 1) for v in tiles]
        return [jnp.where(lane >= 16, moved[t], moved[(t + 2) % 3]) for t in range(3)]

    def packed_turn(colour, edges):
        ex, ey, ez = ([edges[c, t] for t in range(3)] for c in range(3))
        eyx, ezx = next_plane(ey), next_plane(ez)
        fx, fy, fz = [], [], []
        for t in range(3):
            keep = PKEEP[t]
            fx.append((ey[t] - up_lane(ey[t]) + up_row(ez[t]) - ez[t]) * keep)
            fy.append((ez[t] - ezx[t] + up_lane(ex[t]) - ex[t]) * keep)
            fz.append((ex[t] - up_row(ex[t]) + eyx[t] - ey[t]) * keep)
        fyp, fzp = previous_plane(fy), previous_plane(fz)
        for t in range(3):
            U[0, t] = jnp.where(spot == 4, ex[t], roll(fy[t], LANES - 6, 1))
            U[1, t] = jnp.where(spot == 4, ey[t], roll(fx[t], LANES - 6, 1))
            back = (
                fz[t] - down_row(fz[t]) - fy[t] + down_lane(fy[t]),
                fx[t] - down_lane(fx[t]) - fz[t] + fzp[t],
                fy[t] - fyp[t] - fx[t] + down_row(fx[t]),
            )
            for c, old in enumerate((ex[t], ey[t], ez[t])):
                residual = PW[c, t] - back[c] - PW[3, t] * old
                edges[c, t] = old + jnp.where(PW[4 + c, t] == colour + 1.0, residual * PINV[t], 0.0)

    def turn(colour, edges, packed, reach, target=None):
        packed_turn(colour, packed)

        def ends_at(xp):
            t, g = group_of(xp)
            shift = (251 - 16 * g) & (LANES - 1)
            return roll(U[0, t], shift, 1), roll(U[1, t], shift, 1)

        def moved(xp):
            ex, ey, ez = (edges[c, xp] for c in range(3))
            return ex, ey, ez, edges[1, xp + 1], edges[2, xp + 1], up_lane(ex), up_lane(ey)

        def faces(xp, values, fill):
            ex, ey, ez, ey_x, ez_x, ex_z, ey_z = values
            ex_z = jnp.where(lane == LANES - 1, fill[0], ex_z)
            ey_z = jnp.where(lane == LANES - 1, fill[1], ey_z)
            keep = low_rows * x_low(xp)
            fx = (ey - ey_z + up_row(ez) - ez) * keep
            fy = (ez - ez_x + ex_z - ex) * keep
            fz = (ex - up_row(ex) + ey_x - ey) * keep
            return fx, fy, fz

        def planes_turn(planes, carry):
            fyp, fzp = carry
            fills = [ends_at(xp) for xp in planes]
            olds = [moved(xp) for xp in planes]
            fs = [faces(xp, old, fill) for xp, old, fill in zip(planes, olds, fills)]
            backs = [(down_lane(f[0]), down_lane(f[1])) for f in fs]
            values = []
            for xp, old, fill, (fx, fy, fz), (fx_z, fy_z) in zip(planes, olds, fills, fs, backs):
                fx_z = jnp.where(lane == 0, fill[1], fx_z)
                fy_z = jnp.where(lane == 0, fill[0], fy_z)
                back = (
                    fz - down_row(fz) - fy + fy_z,
                    fx - fx_z - fz + fzp,
                    fy - fyp - fx + down_row(fx),
                )
                fyp, fzp = fy, fz
                sigma, inverse = W[3, xp], INV[xp]
                for c in range(3):
                    residual = W[c, xp] - back[c] - sigma * old[c]
                    values.append(
                        old[c] + jnp.where(W[4 + c, xp] == colour + 1.0, residual * inverse, 0.0)
                    )
            for i, xp in enumerate(planes):
                for c in range(3):
                    if target is None:
                        edges[c, xp] = values[3 * i + c]
                    else:
                        target[c, xp, OWN] = values[3 * i + c][OWN]
            return fyp, fzp

        begin = H - reach - 1
        start = faces(begin, moved(begin), ends_at(begin))
        carry = (start[1], start[2])
        every = list(range(H - reach, H + N + reach))
        for i in range(0, len(every), BATCH):
            carry = planes_turn(every[i : i + BATCH], carry)

    turn(1, E, PE, 2)
    turn(2, E, PE, 1)
    turn(3, E, PE, 0, target=E2)

    pack_own(E2, QME, 3)
    copies = exchange(1, E2, QME, QRE)

    top = tab[0]
    for i in range(1, 16):
        top = jnp.maximum(top, tab[i])
    upper = jnp.full((B, LANES), 13.0 * top, jnp.float32)
    ratio = 31.0 / 29.0
    per_centre = (60.0 / 31.0) / upper
    per_half = (60.0 / 29.0) / upper

    @pl.loop(1, B)
    def _(xp):
        t, g = group_of(xp)
        end = roll(PW[2, t], (245 - 16 * g) & (LANES - 1), 1)
        inside = (row_mask * x_mask(xp)) > 0.0
        own = [W[c, xp] for c in range(3)]
        below = [W[0, xp - 1], down_row(own[1]), jnp.where(lane == 0, end, down_lane(own[2]))]
        values = [(below[0] - own[0]) + (below[1] - own[1]) + (below[2] - own[2])]
        values += [0.5 * (own[c] + below[c]) for c in range(3)]
        for f in range(4):
            value = jnp.where(inside, values[f], 0.0)
            NR[f, xp] = value
            value = value * per_centre
            ND[f, xp] = value
            NY[f, xp] = value

    own = [[PW[c, t] for t in range(3)] for c in range(3)]
    below = [
        previous_plane(own[0]),
        [down_row(v) for v in own[1]],
        [down_lane(v) for v in own[2]],
    ]
    for t in range(3):
        values = [sum((below[c][t] - own[c][t]) for c in range(3))]
        values += [0.5 * (own[c][t] + below[c][t]) for c in range(3)]
        for f in range(4):
            value = jnp.where(PMASK[t] > 0.0, values[f], 0.0)
            PR[f, t] = value
            value = value * per_centre
            PD[f, t] = value
            PY[f, t] = value

    rho = 1.0 / ratio
    for n in range(1, NCHEB):
        rho_next = 1.0 / (2.0 * ratio - rho)
        keep_part = rho_next * rho
        new_part = (2.0 * rho_next) * per_half
        rho = rho_next

        @pl.loop(0, 4)
        def _(f, keep_part=keep_part, new_part=new_part):
            mass = jnp.where(f > 0, 1.0, 0.0)
            d = [PD[f, t] for t in range(3)]
            dx = next_plane(d)
            sigma = [PW[3, t] for t in range(3)]
            wx = [sigma[t] * (dx[t] - d[t]) for t in range(3)]
            wxp = previous_plane(wx)
            for t in range(3):
                wy = sigma[t] * (up_row(d[t]) - d[t])
                wz = sigma[t] * (up_lane(d[t]) - d[t])
                UD[f, t] = jnp.where(spot == 4, d[t], roll(wz, LANES - 6, 1))
                applied = (
                    mass * sigma[t] * d[t]
                    + (wxp[t] - wx[t]) + (down_row(wy) - wy) + (down_lane(wz) - wz)
                )
                res = PR[f, t] - applied
                PR[f, t] = res
                new = jnp.where(PMASK[t] > 0.0, keep_part * d[t] + new_part * res, 0.0)
                PD[f, t] = new
                PY[f, t] = PY[f, t] + new

        low, high = n + 1, B - n

        @pl.loop(0, 4)
        def _(f, keep_part=keep_part, new_part=new_part, low=low, high=high):
            mass = jnp.where(f > 0, 1.0, 0.0)
            wxp = W[3, low - 1] * (ND[f, low] - ND[f, low - 1])
            for i in range(low, high, NBATCH):
                planes = list(range(i, min(i + NBATCH, high)))
                ends = []
                for xp in planes:
                    t, g = group_of(xp)
                    ends.append(roll(UD[f, t], (251 - 16 * g) % LANES, 1))
                ds = [ND[f, xp] for xp in planes] + [ND[f, planes[-1] + 1]]
                ups = [up_lane(d) for d in ds[:-1]]
                sigmas = [W[3, xp] for xp in planes]
                wzs = [
                    sigma * (jnp.where(lane == LANES - 1, end, up) - d)
                    for sigma, end, up, d in zip(sigmas, ends, ups, ds)
                ]
                downs = [down_lane(wz) for wz in wzs]
                for j, xp in enumerate(planes):
                    d, sigma, wz = ds[j], sigmas[j], wzs[j]
                    wx = sigma * (ds[j + 1] - d)
                    wy = sigma * (up_row(d) - d)
                    applied = (
                        (mass * sigma) * d + (wxp - wx) + (down_row(wy) - wy)
                        + (jnp.where(lane == 0, ends[j], downs[j]) - wz)
                    )
                    wxp = wx
                    res = NR[f, xp] - applied
                    inside = (row_mask * x_mask(xp)) > 0.0
                    new = jnp.where(inside, keep_part * d + new_part * res, 0.0)
                    NR[f, xp] = res
                    ND[f, xp] = new
                    NY[f, xp] = NY[f, xp] + new

    @pl.loop(0, N)
    def _(x):
        xp = x + H
        t, g = group_of(xp)
        shift = (251 - 16 * g) & (LANES - 1)
        potential = NY[0, xp]
        last_lane = lane == LANES - 1
        pieces = (
            (NY[0, xp + 1], NY[1, xp], NY[1, xp + 1]),
            (up_row(potential), NY[2, xp], up_row(NY[2, xp])),
            (
                jnp.where(last_lane, roll(PY[0, t], shift, 1), up_lane(potential)),
                NY[3, xp],
                jnp.where(last_lane, roll(PY[3, t], shift, 1), up_lane(NY[3, xp])),
            ),
        )
        for c, (above, own_part, next_part) in enumerate(pieces):
            out[c, x] = ((above - potential) + 0.5 * (own_part + next_part))[OWN]

    for copy in copies:
        copy.wait()

    @pl.loop(0, B)
    def _(xp):
        inside = (row_mask * x_mask(xp)) > 0.0
        for c in range(3):
            E2[c, xp] = jnp.where(inside, E2[c, xp], 0.0)

    assemble(E2, QRE, PE2, 3)
    for colour in range(4):
        turn(colour, E2, PE2, 3 - colour)

    @pl.loop(0, N)
    def _(x):
        for c in range(3):
            out[c, x] = out[c, x] + E2[c, x + H, OWN]


def solution(mesh):
    sizes = tuple(mesh.shape[a] for a in AXES)

    def on_device(right_side, labels, colors, table):
        f32 = jnp.float32
        plain = lambda n: pltpu.VMEM((n, B, B, LANES), f32)
        packed = lambda n: pltpu.VMEM((n, 3, B, LANES), f32)
        any_spec = pl.BlockSpec(memory_space=pl.ANY)
        return pl.pallas_call(
            functools.partial(kernel, sizes),
            out_shape=jax.ShapeDtypeStruct(right_side.shape, f32),
            in_specs=[any_spec, any_spec, any_spec, pl.BlockSpec(memory_space=pltpu.SMEM)],
            out_specs=pl.BlockSpec(memory_space=pltpu.VMEM),
            scratch_shapes=[
                pltpu.VMEM((3, N, N, LANES), f32),
                pltpu.VMEM((N, N, LANES), jnp.int32),
                pltpu.VMEM((3, N, N, LANES), jnp.int32),
                plain(7),
                pltpu.VMEM((7, 2, B, LANES), f32),
                pltpu.VMEM((2, 7, 4, B, LANES), f32),
                packed(7),
                pltpu.VMEM((B, B, LANES), f32),
                pltpu.VMEM((3, B, LANES), f32),
                pltpu.VMEM((3, B, LANES), f32),
                pltpu.VMEM((3, B, LANES), f32),
                plain(3),
                packed(3),
                plain(3),
                packed(3),
                pltpu.VMEM((3, 2, B, LANES), f32),
                pltpu.VMEM((2, 3, 4, B, LANES), f32),
                packed(2),
                plain(4),
                plain(4),
                plain(4),
                packed(4),
                packed(4),
                packed(4),
                packed(4),
                pltpu.SemaphoreType.DMA((3,)),
                pltpu.SemaphoreType.DMA((2, len(DIRS))),
                pltpu.SemaphoreType.DMA((2, len(DIRS))),
            ],
            compiler_params=pltpu.CompilerParams(
                collective_id=0, has_side_effects=True, vmem_limit_bytes=40 * 1024 * 1024
            ),
            cost_estimate=pl.CostEstimate(flops=10**8, bytes_accessed=2 * 10**6, transcendentals=0),
        )(right_side, labels, colors, table)

    in_specs = (P(None, "gx", "gy", "gz"), P("gx", "gy", "gz"), P(None, "gx", "gy", "gz"), P())
    return jax.shard_map(
        on_device, mesh=mesh, in_specs=in_specs, out_specs=P(None, "gx", "gy", "gz"), check_vma=False
    )
```

```python
import functools
import itertools

import jax
import jax.numpy as jnp
from jax import lax
from jax.experimental import pallas as pl
from jax.experimental.pallas import tpu as pltpu
from jax.sharding import PartitionSpec as P

NSWEEP = 2
NCOL = 4
NCHEB = 4
AXES = ("gx", "gy", "gz")

H = 4
N = 16
B = N + 2 * H
LANES = 128
BATCH = 5
NBATCH = 7
OWN = slice(H, H + N)
DIRS = [d for d in itertools.product((-1, 0, 1), repeat=3) if 0 < sum(map(abs, d)) < 3]
RELAYS = [(dx, dy) for dx in (-1, 1) for dy in (-1, 1)]


def roll(values, shift, axis):
    return pltpu.roll(values, shift, axis)


def down_lane(values):
    return roll(values, 1, 1)


def up_lane(values):
    return roll(values, LANES - 1, 1)


def down_row(values):
    return roll(values, 1, 0)


def up_row(values):
    return roll(values, B - 1, 0)


def group_of(xp):
    ring = (xp + (B - H)) % B if isinstance(xp, int) else jnp.where(xp >= H, xp - H, xp + (B - H))
    return ring >> 3, ring & 7


def select_table(labels, table):
    level = [table[i] for i in range(16)]
    for bit in range(4):
        odd = (labels & (1 << bit)) != 0
        level = [jnp.where(odd, level[i + 1], level[i]) for i in range(0, len(level), 2)]
    return level[0]


def kernel(
    sizes,
    r_hbm, lab_hbm, col_hbm, tab_hbm,
    out,
    r_in, lab_in, col_in, tab,
    W, QM, QR, PW, INV, PINV, PMASK, PKEEP,
    E, PE, E2, PE2, QME, QRE, U,
    NR, ND, NY, PR, PD, PY, UD,
    xs_w, xr_w, xp_w, xc_w, xs_e, xr_e, xp_e, xc_e,
    in_sem, ssem, rsem,
):
    XW, XE = (xs_w, xr_w, xp_w, xc_w), (xs_e, xr_e, xp_e, xc_e)
    here = [lax.axis_index(a) for a in AXES]
    places = [
        {
            0: here[i],
            1: jnp.where(here[i] == sizes[i] - 1, 0, here[i] + 1),
            -1: jnp.where(here[i] == 0, sizes[i] - 1, here[i] - 1),
        }
        for i in range(3)
    ]

    def neighbour(d):
        return tuple(places[i][d[i]] for i in range(3))

    def exists(d):
        found = None
        for i in range(3):
            if d[i]:
                one = here[i] < sizes[i] - 1 if d[i] > 0 else here[i] > 0
                found = one if found is None else jnp.logical_and(found, one)
        return found

    def opposite(d):
        return tuple(-step for step in d)

    loads = [
        pltpu.make_async_copy(src, dst, in_sem.at[i])
        for i, (src, dst) in enumerate(
            ((tab_hbm, tab), (lab_hbm, lab_in), (r_hbm, r_in), (col_hbm, col_in))
        )
    ]
    for load in loads:
        load.start()
    barrier = pltpu.get_barrier_semaphore()
    around = jnp.int32(0)
    for d in DIRS:
        around = around + exists(d).astype(jnp.int32)

        @pl.when(exists(d))
        def _(d=d):
            pl.semaphore_signal(
                barrier, inc=1, device_id=neighbour(d), device_id_type=pl.DeviceIdType.MESH
            )


    first = [jnp.where(here[i] > 0, 1.0, 0.0).astype(jnp.float32) for i in range(3)]
    last = [jnp.where(here[i] < sizes[i] - 1, 1.0, 0.0).astype(jnp.float32) for i in range(3)]
    lane = lax.broadcasted_iota(jnp.int32, (B, LANES), 1)
    row = lax.broadcasted_iota(jnp.int32, (B, LANES), 0)
    spot = lane % 16
    low_rows = jnp.where(row < H, first[1], 1.0)
    row_mask = low_rows * jnp.where(row >= H + N, last[1], 1.0)
    low_ends = jnp.where((spot >= 8) & (spot < 12), first[2], 1.0) * low_rows
    ends = jnp.where((spot >= 4) & (spot < 8), last[2], 1.0) * low_ends * jnp.where(
        row >= H + N, last[1], 1.0
    )
    before = jnp.where(lane >= 64, first[0], 1.0)
    after = jnp.where(lane < 64, last[0], 1.0)
    for t in range(3):
        PKEEP[t] = low_ends * before if t == 2 else low_ends
        PMASK[t] = ends * before * after if t == 2 else ends

    def x_low(xp):
        if isinstance(xp, int):
            return first[0] if xp < H else 1.0
        return jnp.where(xp >= H, 1.0, first[0])

    def x_mask(xp):
        if isinstance(xp, int):
            return last[0] if xp >= H + N else x_low(xp)
        return x_low(xp) * jnp.where(xp < H + N, 1.0, last[0])

    for load in loads:
        load.wait()

    @pl.loop(0, N, unroll=4)
    def _(x):
        W[3, x + H, OWN] = select_table(lab_in[x], tab)
        for c in range(3):
            W[c, x + H, OWN] = r_in[c, x]
            W[4 + c, x + H, OWN] = col_in[c, x].astype(jnp.float32) + 1.0

    def pack_own(src, dst, fields):
        narrow = lax.broadcasted_iota(jnp.int32, (N, LANES), 1) // 16

        @pl.loop(0, fields)
        def _(f):
            for t in range(2):
                total = None
                for g in range(8):
                    piece = roll(src[f, H + 8 * t + g, OWN], 16 * g + 4, 1)
                    total = piece if g == 0 else jnp.where(narrow == g, piece, total)
                dst[f, t, OWN] = total

    pack_own(W, QM, 7)
    pl.semaphore_wait(barrier, around)

    def span(d, side):
        if d == 0:
            return slice(H, H + N)
        low = (d > 0) == (side == "dst")
        if side == "dst":
            return slice(0, H) if low else slice(H + N, B)
        return slice(H, 2 * H) if d < 0 else slice(N, N + H)

    def merge(parts, half):
        shape = parts[0].shape
        lanes = lax.broadcasted_iota(jnp.int32, shape, 1)
        pair = lanes % 16 < 8
        out = jnp.where(pair, parts[0], roll(parts[1], 8, 1))
        other = roll(parts[2], 64, 1)
        if len(parts) > 3:
            other = jnp.where(pair, other, roll(parts[3], 72, 1))
        return jnp.where((lanes < 64) == (half == 0), out, other)

    def groups(fields):
        return [list(range(i, min(i + 4, fields))) for i in range(0, fields, 4)]

    def remote(phase, i, src, dst, d):
        return pltpu.make_async_remote_copy(
            src_ref=src,
            dst_ref=dst,
            send_sem=ssem.at[phase, i],
            recv_sem=rsem.at[phase, i],
            device_id=neighbour(d),
            device_id_type=pl.DeviceIdType.MESH,
        )

    def exchange(phase, main, packed, received, sides, fields):
        sent, got = sides[0], sides[1]
        tiles = len(groups(fields))
        for h in range(2):
            for k, group in enumerate(groups(fields)):
                sent[h, k] = merge([packed[f, h, OWN] for f in group], h)
        copies = {}
        for i, d in enumerate(DIRS):
            rows_src, rows_dst = span(d[1], "src"), span(d[1], "dst")
            if d[2] == 0:
                src = main.at[:, span(d[0], "src"), rows_src]
                dst = main.at[:, span(d[0], "dst"), rows_dst]
            elif d[0] == 0:
                src = packed.at[:, :, rows_src]
                dst = received.at[1 if d[2] > 0 else 0, :, :, rows_dst]
            else:
                h = 1 if d[0] > 0 else 0
                src = sent.at[h]
                dst = got.at[1 if d[2] > 0 else 0, h, :, rows_dst]
            copies[d] = remote(phase, i, src, dst, d)
        rank = lambda d: (abs(d[1]) * abs(d[2]) == 0, abs(d[0]) * abs(d[2]) == 0, -abs(d[0]), -abs(d[2]))
        for d in sorted(DIRS, key=rank):
            pl.when(exists(d))(copies[d].start)
        return copies

    def relay(phase, copies, received, sides, fields):
        passed, corner = sides[2], sides[3]
        for d in DIRS:
            if d[0] == 0 and d[1] and d[2]:
                pl.when(exists(opposite(d)))(copies[d].wait_recv)
        narrow = lax.broadcasted_iota(jnp.int32, (H, LANES), 1) % 16 < 4
        for i, (dx, dy) in enumerate(RELAYS):
            h, rows = (1 if dx > 0 else 0), (slice(0, H) if dy < 0 else slice(H + N, B))
            for k, group in enumerate(groups(fields)):
                parts = [jnp.where(narrow, received[1, f, h, rows], received[0, f, h, rows]) for f in group]
                passed[i, k, 0:H] = merge(parts, h)
            copy = remote(
                phase, len(DIRS) + i, passed.at[i, :, 0:H], corner.at[h, :, rows], (dx, 0, 0)
            )
            pl.when(exists((dx, 0, 0)))(copy.start)
            copies[(dx, dy)] = copy

    def finish(copies):
        for d, copy in copies.items():
            way = d if len(d) == 3 else (d[0], 0, 0)
            if len(d) == 2 or d[0] or not (d[1] and d[2]):
                pl.when(exists(opposite(way)))(copy.wait_recv)
            pl.when(exists(way))(copy.wait_send)

    def assemble(src, received, sides, dst, fields):
        got, corner = sides[1], sides[3]
        edge_rows = (row < H) | (row >= H + N)
        left = lane < 64
        across = [[None] * fields, [None] * fields]
        for side in range(2):
            for k, group in enumerate(groups(fields)):
                high, low = (jnp.where(edge_rows, corner[h, k], got[side, h, k]) for h in range(2))
                near, far = jnp.where(left, high, low), jnp.where(left, low, high)
                moved = (near, roll(near, 120, 1), roll(far, 64, 1), roll(far, 56, 1))
                for f, value in zip(group, moved):
                    across[side][f] = value
        for f in range(fields):
            for t in range(3):
                own = None
                for g in range(8):
                    x = (8 * t + g + H) % B
                    piece = roll(src[f, x], 16 * g + 4, 1)
                    own = piece if g == 0 else jnp.where(lane // 16 == g, piece, own)
                if t < 2:
                    high, low = received[0, f, t], received[1, f, t]
                else:
                    high, low = across[0][f], across[1][f]
                upper = jnp.where(spot < 4, own, high)
                lower = roll(jnp.where(spot < 4, low, own), 8, 1)
                dst[f, t] = jnp.where(PMASK[t] > 0.0, jnp.where(spot < 8, upper, lower), 0.0)

    copies = exchange(0, W, QM, QR, XW, 7)
    relay(0, copies, QR, XW, 7)
    finish(copies)

    @pl.loop(0, B, unroll=4)
    def _(xp):
        inside = (row_mask * x_mask(xp)) > 0.0
        for f in range(7):
            W[f, xp] = jnp.where(inside, W[f, xp], 0.0)
        inverse = 1.0 / (16.0 + W[3, xp])
        INV[xp] = inverse
        for c in range(3):
            E[c, xp] = jnp.where(W[4 + c, xp] == 1.0, W[c, xp] * inverse, 0.0)

    assemble(W, QR, XW, PW, 7)
    for t in range(3):
        PINV[t] = 1.0 / (16.0 + PW[3, t])
        for c in range(3):
            PE[c, t] = jnp.where(PW[4 + c, t] == 1.0, PW[c, t] * PINV[t], 0.0)

    def next_plane(tiles):
        moved = [roll(v, LANES - 16, 1) for v in tiles]
        return [jnp.where(lane < LANES - 16, moved[t], moved[(t + 1) % 3]) for t in range(3)]

    def previous_plane(tiles):
        moved = [roll(v, 16, 1) for v in tiles]
        return [jnp.where(lane >= 16, moved[t], moved[(t + 2) % 3]) for t in range(3)]

    def packed_turn(colour, edges):
        ex, ey, ez = ([edges[c, t] for t in range(3)] for c in range(3))
        eyx, ezx = next_plane(ey), next_plane(ez)
        fx, fy, fz = [], [], []
        for t in range(3):
            keep = PKEEP[t]
            fx.append((ey[t] - up_lane(ey[t]) + up_row(ez[t]) - ez[t]) * keep)
            fy.append((ez[t] - ezx[t] + up_lane(ex[t]) - ex[t]) * keep)
            fz.append((ex[t] - up_row(ex[t]) + eyx[t] - ey[t]) * keep)
        fyp, fzp = previous_plane(fy), previous_plane(fz)
        for t in range(3):
            U[0, t] = jnp.where(spot == 4, ex[t], roll(fy[t], LANES - 6, 1))
            U[1, t] = jnp.where(spot == 4, ey[t], roll(fx[t], LANES - 6, 1))
            back = (
                fz[t] - down_row(fz[t]) - fy[t] + down_lane(fy[t]),
                fx[t] - down_lane(fx[t]) - fz[t] + fzp[t],
                fy[t] - fyp[t] - fx[t] + down_row(fx[t]),
            )
            for c, old in enumerate((ex[t], ey[t], ez[t])):
                residual = PW[c, t] - back[c] - PW[3, t] * old
                edges[c, t] = old + jnp.where(PW[4 + c, t] == colour + 1.0, residual * PINV[t], 0.0)

    def turn(colour, edges, packed, reach, target=None):
        packed_turn(colour, packed)

        def ends_at(xp):
            t, g = group_of(xp)
            shift = (251 - 16 * g) & (LANES - 1)
            return roll(U[0, t], shift, 1), roll(U[1, t], shift, 1)

        def moved(xp):
            ex, ey, ez = (edges[c, xp] for c in range(3))
            return ex, ey, ez, edges[1, xp + 1], edges[2, xp + 1], up_lane(ex), up_lane(ey)

        def faces(xp, values, fill):
            ex, ey, ez, ey_x, ez_x, ex_z, ey_z = values
            ex_z = jnp.where(lane == LANES - 1, fill[0], ex_z)
            ey_z = jnp.where(lane == LANES - 1, fill[1], ey_z)
            keep = low_rows * x_low(xp)
            fx = (ey - ey_z + up_row(ez) - ez) * keep
            fy = (ez - ez_x + ex_z - ex) * keep
            fz = (ex - up_row(ex) + ey_x - ey) * keep
            return fx, fy, fz

        def planes_turn(planes, carry):
            fyp, fzp = carry
            fills = [ends_at(xp) for xp in planes]
            olds = [moved(xp) for xp in planes]
            fs = [faces(xp, old, fill) for xp, old, fill in zip(planes, olds, fills)]
            backs = [(down_lane(f[0]), down_lane(f[1])) for f in fs]
            values = []
            for xp, old, fill, (fx, fy, fz), (fx_z, fy_z) in zip(planes, olds, fills, fs, backs):
                fx_z = jnp.where(lane == 0, fill[1], fx_z)
                fy_z = jnp.where(lane == 0, fill[0], fy_z)
                back = (
                    fz - down_row(fz) - fy + fy_z,
                    fx - fx_z - fz + fzp,
                    fy - fyp - fx + down_row(fx),
                )
                fyp, fzp = fy, fz
                sigma, inverse = W[3, xp], INV[xp]
                for c in range(3):
                    residual = W[c, xp] - back[c] - sigma * old[c]
                    values.append(
                        old[c] + jnp.where(W[4 + c, xp] == colour + 1.0, residual * inverse, 0.0)
                    )
            for i, xp in enumerate(planes):
                for c in range(3):
                    if target is None:
                        edges[c, xp] = values[3 * i + c]
                    else:
                        target[c, xp, OWN] = values[3 * i + c][OWN]
            return fyp, fzp

        begin = H - reach - 1
        start = faces(begin, moved(begin), ends_at(begin))
        carry = (start[1], start[2])
        every = list(range(H - reach, H + N + reach))
        for i in range(0, len(every), BATCH):
            carry = planes_turn(every[i : i + BATCH], carry)

    turn(1, E, PE, 2)
    turn(2, E, PE, 1)
    turn(3, E, PE, 0, target=E2)

    pack_own(E2, QME, 3)
    copies = exchange(1, E2, QME, QRE, XE, 3)

    top = tab[0]
    for i in range(1, 16):
        top = jnp.maximum(top, tab[i])
    upper = jnp.full((B, LANES), 13.0 * top, jnp.float32)
    ratio = 31.0 / 29.0
    per_centre = (60.0 / 31.0) / upper
    per_half = (60.0 / 29.0) / upper

    @pl.loop(1, B, unroll=6)
    def _(xp):
        t, g = group_of(xp)
        end = roll(PW[2, t], (245 - 16 * g) & (LANES - 1), 1)
        inside = (row_mask * x_mask(xp)) > 0.0
        own = [W[c, xp] for c in range(3)]
        below = [W[0, xp - 1], down_row(own[1]), jnp.where(lane == 0, end, down_lane(own[2]))]
        values = [(below[0] - own[0]) + (below[1] - own[1]) + (below[2] - own[2])]
        values += [0.5 * (own[c] + below[c]) for c in range(3)]
        for f in range(4):
            value = jnp.where(inside, values[f], 0.0)
            NR[f, xp] = value
            value = value * per_centre
            ND[f, xp] = value
            NY[f, xp] = value

    own = [[PW[c, t] for t in range(3)] for c in range(3)]
    below = [
        previous_plane(own[0]),
        [down_row(v) for v in own[1]],
        [down_lane(v) for v in own[2]],
    ]
    for t in range(3):
        values = [sum((below[c][t] - own[c][t]) for c in range(3))]
        values += [0.5 * (own[c][t] + below[c][t]) for c in range(3)]
        for f in range(4):
            value = jnp.where(PMASK[t] > 0.0, values[f], 0.0)
            PR[f, t] = value
            value = value * per_centre
            PD[f, t] = value
            PY[f, t] = value

    rho = 1.0 / ratio
    for n in range(1, NCHEB):
        rho_next = 1.0 / (2.0 * ratio - rho)
        keep_part = rho_next * rho
        new_part = (2.0 * rho_next) * per_half
        rho = rho_next

        @pl.loop(0, 4)
        def _(f, keep_part=keep_part, new_part=new_part):
            mass = jnp.where(f > 0, 1.0, 0.0)
            d = [PD[f, t] for t in range(3)]
            dx = next_plane(d)
            sigma = [PW[3, t] for t in range(3)]
            wx = [sigma[t] * (dx[t] - d[t]) for t in range(3)]
            wxp = previous_plane(wx)
            for t in range(3):
                wy = sigma[t] * (up_row(d[t]) - d[t])
                wz = sigma[t] * (up_lane(d[t]) - d[t])
                UD[f, t] = jnp.where(spot == 4, d[t], roll(wz, LANES - 6, 1))
                applied = (
                    mass * sigma[t] * d[t]
                    + (wxp[t] - wx[t]) + (down_row(wy) - wy) + (down_lane(wz) - wz)
                )
                res = PR[f, t] - applied
                PR[f, t] = res
                new = jnp.where(PMASK[t] > 0.0, keep_part * d[t] + new_part * res, 0.0)
                PD[f, t] = new
                PY[f, t] = PY[f, t] + new

        low, high = n + 1, B - n

        @pl.loop(0, 4)
        def _(f, keep_part=keep_part, new_part=new_part, low=low, high=high):
            mass = jnp.where(f > 0, 1.0, 0.0)
            wxp = W[3, low - 1] * (ND[f, low] - ND[f, low - 1])
            for i in range(low, high, NBATCH):
                planes = list(range(i, min(i + NBATCH, high)))
                ends = []
                for xp in planes:
                    t, g = group_of(xp)
                    ends.append(roll(UD[f, t], (251 - 16 * g) % LANES, 1))
                ds = [ND[f, xp] for xp in planes] + [ND[f, planes[-1] + 1]]
                ups = [up_lane(d) for d in ds[:-1]]
                sigmas = [W[3, xp] for xp in planes]
                wzs = [
                    sigma * (jnp.where(lane == LANES - 1, end, up) - d)
                    for sigma, end, up, d in zip(sigmas, ends, ups, ds)
                ]
                downs = [down_lane(wz) for wz in wzs]
                for j, xp in enumerate(planes):
                    d, sigma, wz = ds[j], sigmas[j], wzs[j]
                    wx = sigma * (ds[j + 1] - d)
                    wy = sigma * (up_row(d) - d)
                    applied = (
                        (mass * sigma) * d + (wxp - wx) + (down_row(wy) - wy)
                        + (jnp.where(lane == 0, ends[j], downs[j]) - wz)
                    )
                    wxp = wx
                    res = NR[f, xp] - applied
                    inside = (row_mask * x_mask(xp)) > 0.0
                    new = jnp.where(inside, keep_part * d + new_part * res, 0.0)
                    NR[f, xp] = res
                    ND[f, xp] = new
                    NY[f, xp] = NY[f, xp] + new

        if n == 1:
            relay(1, copies, QRE, XE, 3)

    @pl.loop(0, N, unroll=4)
    def _(x):
        xp = x + H
        t, g = group_of(xp)
        shift = (251 - 16 * g) & (LANES - 1)
        potential = NY[0, xp]
        last_lane = lane == LANES - 1
        pieces = (
            (NY[0, xp + 1], NY[1, xp], NY[1, xp + 1]),
            (up_row(potential), NY[2, xp], up_row(NY[2, xp])),
            (
                jnp.where(last_lane, roll(PY[0, t], shift, 1), up_lane(potential)),
                NY[3, xp],
                jnp.where(last_lane, roll(PY[3, t], shift, 1), up_lane(NY[3, xp])),
            ),
        )
        for c, (above, own_part, next_part) in enumerate(pieces):
            out[c, x] = ((above - potential) + 0.5 * (own_part + next_part))[OWN]

    finish(copies)

    @pl.loop(0, B, unroll=4)
    def _(xp):
        inside = (row_mask * x_mask(xp)) > 0.0
        for c in range(3):
            E2[c, xp] = jnp.where(inside, E2[c, xp], 0.0)

    assemble(E2, QRE, XE, PE2, 3)
    for colour in range(4):
        turn(colour, E2, PE2, 3 - colour)

    @pl.loop(0, N, unroll=4)
    def _(x):
        for c in range(3):
            out[c, x] = out[c, x] + E2[c, x + H, OWN]


def solution(mesh):
    sizes = tuple(mesh.shape[a] for a in AXES)

    def on_device(right_side, labels, colors, table):
        f32 = jnp.float32
        plain = lambda n: pltpu.VMEM((n, B, B, LANES), f32)
        packed = lambda n: pltpu.VMEM((n, 3, B, LANES), f32)
        across = lambda k: [
            pltpu.VMEM((2, k, N, LANES), f32),
            pltpu.VMEM((2, 2, k, B, LANES), f32),
            pltpu.VMEM((len(RELAYS), k, 8, LANES), f32),
            pltpu.VMEM((2, k, B, LANES), f32),
        ]
        any_spec = pl.BlockSpec(memory_space=pltpu.HBM)
        return pl.pallas_call(
            functools.partial(kernel, sizes),
            out_shape=jax.ShapeDtypeStruct(right_side.shape, f32),
            in_specs=[any_spec] * 4,
            out_specs=pl.BlockSpec(memory_space=pltpu.VMEM),
            scratch_shapes=[
                pltpu.VMEM((3, N, N, LANES), f32),
                pltpu.VMEM((N, N, LANES), jnp.int32),
                pltpu.VMEM((3, N, N, LANES), jnp.int32),
                pltpu.SMEM((16,), f32),
                plain(7),
                pltpu.VMEM((7, 2, B, LANES), f32),
                pltpu.VMEM((2, 7, 2, B, LANES), f32),
                packed(7),
                pltpu.VMEM((B, B, LANES), f32),
                pltpu.VMEM((3, B, LANES), f32),
                pltpu.VMEM((3, B, LANES), f32),
                pltpu.VMEM((3, B, LANES), f32),
                plain(3),
                packed(3),
                plain(3),
                packed(3),
                pltpu.VMEM((3, 2, B, LANES), f32),
                pltpu.VMEM((2, 3, 2, B, LANES), f32),
                packed(2),
                plain(4),
                plain(4),
                plain(4),
                packed(4),
                packed(4),
                packed(4),
                packed(4),
                *across(2),
                *across(1),
                pltpu.SemaphoreType.DMA((4,)),
                pltpu.SemaphoreType.DMA((2, len(DIRS) + len(RELAYS))),
                pltpu.SemaphoreType.DMA((2, len(DIRS) + len(RELAYS))),
            ],
            compiler_params=pltpu.CompilerParams(
                collective_id=0, has_side_effects=True, vmem_limit_bytes=63 * 1024 * 1024
            ),
            cost_estimate=pl.CostEstimate(flops=10**8, bytes_accessed=2 * 10**6, transcendentals=0),
        )(right_side, labels, colors, table)

    in_specs = (P(None, "gx", "gy", "gz"), P("gx", "gy", "gz"), P(None, "gx", "gy", "gz"), P())
    return jax.shard_map(
        on_device, mesh=mesh, in_specs=in_specs, out_specs=P(None, "gx", "gy", "gz"), check_vma=False
    )
```

```python
import functools
import itertools

import jax
import jax.numpy as jnp
from jax import lax
from jax.experimental import pallas as pl
from jax.experimental.pallas import tpu as pltpu
from jax.sharding import PartitionSpec as P

NSWEEP = 2
NCOL = 4
NCHEB = 4
AXES = ("gx", "gy", "gz")

H = 4
N = 16
B = N + 2 * H
LANES = 128
BATCH = 5
NBATCH = 7
OWN = slice(H, H + N)
DIRS = [d for d in itertools.product((-1, 0, 1), repeat=3) if 0 < sum(map(abs, d)) < 3]
RELAYS = [(dx, dy) for dx in (-1, 1) for dy in (-1, 1)]


def roll(values, shift, axis):
    return pltpu.roll(values, shift, axis)


def down_lane(values):
    return roll(values, 1, 1)


def up_lane(values):
    return roll(values, LANES - 1, 1)


def down_row(values):
    return roll(values, 1, 0)


def up_row(values):
    return roll(values, B - 1, 0)


def group_of(xp):
    ring = (xp + (B - H)) % B if isinstance(xp, int) else jnp.where(xp >= H, xp - H, xp + (B - H))
    return ring >> 3, ring & 7


def select_table(labels, table):
    level = [table[i] for i in range(16)]
    for bit in range(4):
        odd = (labels & (1 << bit)) != 0
        level = [jnp.where(odd, level[i + 1], level[i]) for i in range(0, len(level), 2)]
    return level[0]


def kernel(
    sizes,
    r_hbm, lab_hbm, col_hbm, tab_hbm,
    out,
    r_in, lab_in, col_in, tab,
    W, QM, QR, PW, INV, PINV, PMASK, PKEEP,
    E, PE, E2, PE2, QME, QRE, U,
    NR, ND, NY, PR, PD, PY, UD,
    xs_w, xr_w, xp_w, xc_w, zs_w, xs_e, xr_e, xp_e, xc_e, zs_e,
    in_sem, ssem, rsem,
):
    XW, XE = (xs_w, xr_w, xp_w, xc_w, zs_w), (xs_e, xr_e, xp_e, xc_e, zs_e)
    here = [lax.axis_index(a) for a in AXES]
    places = [
        {
            0: here[i],
            1: jnp.where(here[i] == sizes[i] - 1, 0, here[i] + 1),
            -1: jnp.where(here[i] == 0, sizes[i] - 1, here[i] - 1),
        }
        for i in range(3)
    ]

    def neighbour(d):
        return tuple(places[i][d[i]] for i in range(3))

    def exists(d):
        found = None
        for i in range(3):
            if d[i]:
                one = here[i] < sizes[i] - 1 if d[i] > 0 else here[i] > 0
                found = one if found is None else jnp.logical_and(found, one)
        return found

    def opposite(d):
        return tuple(-step for step in d)

    loads = [
        pltpu.make_async_copy(src, dst, in_sem.at[i])
        for i, (src, dst) in enumerate(
            ((tab_hbm, tab), (lab_hbm, lab_in), (r_hbm, r_in), (col_hbm, col_in))
        )
    ]
    for load in loads:
        load.start()
    barrier = pltpu.get_barrier_semaphore()
    around = jnp.int32(0)
    for d in DIRS:
        around = around + exists(d).astype(jnp.int32)

        @pl.when(exists(d))
        def _(d=d):
            pl.semaphore_signal(
                barrier, inc=1, device_id=neighbour(d), device_id_type=pl.DeviceIdType.MESH
            )


    first = [jnp.where(here[i] > 0, 1.0, 0.0).astype(jnp.float32) for i in range(3)]
    last = [jnp.where(here[i] < sizes[i] - 1, 1.0, 0.0).astype(jnp.float32) for i in range(3)]
    lane = lax.broadcasted_iota(jnp.int32, (B, LANES), 1)
    row = lax.broadcasted_iota(jnp.int32, (B, LANES), 0)
    spot = lane % 16
    low_rows = jnp.where(row < H, first[1], 1.0)
    row_mask = low_rows * jnp.where(row >= H + N, last[1], 1.0)
    low_ends = jnp.where((spot >= 8) & (spot < 12), first[2], 1.0) * low_rows
    ends = jnp.where((spot >= 4) & (spot < 8), last[2], 1.0) * low_ends * jnp.where(
        row >= H + N, last[1], 1.0
    )
    before = jnp.where(lane >= 64, first[0], 1.0)
    after = jnp.where(lane < 64, last[0], 1.0)
    for t in range(3):
        PKEEP[t] = low_ends * before if t == 2 else low_ends
        PMASK[t] = ends * before * after if t == 2 else ends

    def x_low(xp):
        if isinstance(xp, int):
            return first[0] if xp < H else 1.0
        return jnp.where(xp >= H, 1.0, first[0])

    def x_mask(xp):
        if isinstance(xp, int):
            return last[0] if xp >= H + N else x_low(xp)
        return x_low(xp) * jnp.where(xp < H + N, 1.0, last[0])

    for load in loads:
        load.wait()

    @pl.loop(0, N, unroll=4)
    def _(x):
        W[3, x + H, OWN] = select_table(lab_in[x], tab)
        for c in range(3):
            W[c, x + H, OWN] = r_in[c, x]
            W[4 + c, x + H, OWN] = col_in[c, x].astype(jnp.float32) + 1.0

    def pack_own(src, dst, fields):
        narrow = lax.broadcasted_iota(jnp.int32, (N, LANES), 1) // 16

        @pl.loop(0, fields)
        def _(f):
            for t in range(2):
                total = None
                for g in range(8):
                    piece = roll(src[f, H + 8 * t + g, OWN], 16 * g + 4, 1)
                    total = piece if g == 0 else jnp.where(narrow == g, piece, total)
                dst[f, t, OWN] = total

    pack_own(W, QM, 7)

    def span(d, side):
        if d == 0:
            return slice(H, H + N)
        low = (d > 0) == (side == "dst")
        if side == "dst":
            return slice(0, H) if low else slice(H + N, B)
        return slice(H, 2 * H) if d < 0 else slice(N, N + H)

    def merge(parts, half):
        shape = parts[0].shape
        lanes = lax.broadcasted_iota(jnp.int32, shape, 1)
        pair = lanes % 16 < 8
        out = jnp.where(pair, parts[0], roll(parts[1], 8, 1))
        other = roll(parts[2], 64, 1)
        if len(parts) > 3:
            other = jnp.where(pair, other, roll(parts[3], 72, 1))
        return jnp.where((lanes < 64) == (half == 0), out, other)

    def merge_quads(parts, base):
        quad = lax.broadcasted_iota(jnp.int32, parts[0].shape, 1) % 16 // 4
        out = parts[0]
        for i, part in enumerate(parts[1:], 1):
            out = jnp.where(quad == (base + i) % 4, roll(part, 4 * i, 1), out)
        return out

    def split_quad(received, side, f, t, rows):
        value = received[side, f // 4, t, rows]
        return value if f % 4 == 0 else roll(value, LANES - 4 * (f % 4), 1)

    def groups(fields):
        return [list(range(i, min(i + 4, fields))) for i in range(0, fields, 4)]

    def remote(phase, i, src, dst, d):
        return pltpu.make_async_remote_copy(
            src_ref=src,
            dst_ref=dst,
            send_sem=ssem.at[phase, i],
            recv_sem=rsem.at[phase, i],
            device_id=neighbour(d),
            device_id_type=pl.DeviceIdType.MESH,
        )

    def prepare(packed, sides, fields):
        for h in range(2):
            for k, group in enumerate(groups(fields)):
                parts = [packed[f, h, OWN] for f in group]
                sides[0][h, k] = merge(parts, h)
                for side in range(2):
                    sides[4][side, k, h] = merge_quads(parts, side)

    def exchange(phase, main, received, sides):
        sent, got = sides[0], sides[1]
        copies = {}
        for i, d in enumerate(DIRS):
            rows_src, rows_dst = span(d[1], "src"), span(d[1], "dst")
            if d[2] == 0:
                src = main.at[:, span(d[0], "src"), rows_src]
                dst = main.at[:, span(d[0], "dst"), rows_dst]
            elif d[0] == 0:
                src = sides[4].at[0 if d[2] > 0 else 1, :, :, slice(rows_src.start - H, rows_src.stop - H)]
                dst = received.at[1 if d[2] > 0 else 0, :, :, rows_dst]
            else:
                h = 1 if d[0] > 0 else 0
                src = sent.at[h]
                dst = got.at[1 if d[2] > 0 else 0, h, :, rows_dst]
            copies[d] = remote(phase, i, src, dst, d)
        turns = [(0, 1, 1), (1, 0, 1), (1, 1, 0), (0, 1, 0), (0, 0, 1), (1, 0, 0)]
        rank = lambda d: turns.index(tuple(map(abs, d)))
        for d in sorted(DIRS, key=rank):
            pl.when(exists(d))(copies[d].start)
        return copies

    def relay(phase, copies, received, sides, fields):
        passed, corner = sides[2], sides[3]
        for d in DIRS:
            if d[0] == 0 and d[1] and d[2]:
                pl.when(exists(opposite(d)))(copies[d].wait_recv)
        narrow = lax.broadcasted_iota(jnp.int32, (H, LANES), 1) % 16 < 4
        for i, (dx, dy) in enumerate(RELAYS):
            h, rows = (1 if dx > 0 else 0), (slice(0, H) if dy < 0 else slice(H + N, B))
            for k, group in enumerate(groups(fields)):
                parts = [
                    jnp.where(
                        narrow,
                        split_quad(received, 1, f, h, rows),
                        split_quad(received, 0, f, h, rows),
                    )
                    for f in group
                ]
                passed[i, k, 0:H] = merge(parts, h)
            copy = remote(
                phase, len(DIRS) + i, passed.at[i, :, 0:H], corner.at[h, :, rows], (dx, 0, 0)
            )
            pl.when(exists((dx, 0, 0)))(copy.start)
            copies[(dx, dy)] = copy

    def finish(copies):
        for d, copy in copies.items():
            way = d if len(d) == 3 else (d[0], 0, 0)
            if len(d) == 2 or d[0] or not (d[1] and d[2]):
                pl.when(exists(opposite(way)))(copy.wait_recv)
            pl.when(exists(way))(copy.wait_send)

    def assemble(src, received, sides, dst, fields):
        got, corner = sides[1], sides[3]
        edge_rows = (row < H) | (row >= H + N)
        left = lane < 64
        across = [[None] * fields, [None] * fields]
        for side in range(2):
            for k, group in enumerate(groups(fields)):
                high, low = (jnp.where(edge_rows, corner[h, k], got[side, h, k]) for h in range(2))
                near, far = jnp.where(left, high, low), jnp.where(left, low, high)
                moved = (near, roll(near, 120, 1), roll(far, 64, 1), roll(far, 56, 1))
                for f, value in zip(group, moved):
                    across[side][f] = value
        for f in range(fields):
            for t in range(3):
                own = None
                for g in range(8):
                    x = (8 * t + g + H) % B
                    piece = roll(src[f, x], 16 * g + 4, 1)
                    own = piece if g == 0 else jnp.where(lane // 16 == g, piece, own)
                if t < 2:
                    high, low = (split_quad(received, side, f, t, slice(None)) for side in range(2))
                else:
                    high, low = across[0][f], across[1][f]
                upper = jnp.where(spot < 4, own, high)
                lower = roll(jnp.where(spot < 4, low, own), 8, 1)
                dst[f, t] = jnp.where(PMASK[t] > 0.0, jnp.where(spot < 8, upper, lower), 0.0)

    prepare(QM, XW, 7)
    pl.semaphore_wait(barrier, around)
    copies = exchange(0, W, QR, XW)
    relay(0, copies, QR, XW, 7)
    finish(copies)

    @pl.loop(0, B, unroll=4)
    def _(xp):
        inside = (row_mask * x_mask(xp)) > 0.0
        for f in range(7):
            W[f, xp] = jnp.where(inside, W[f, xp], 0.0)
        inverse = 1.0 / (16.0 + W[3, xp])
        INV[xp] = inverse
        for c in range(3):
            E[c, xp] = jnp.where(W[4 + c, xp] == 1.0, W[c, xp] * inverse, 0.0)

    assemble(W, QR, XW, PW, 7)
    for t in range(3):
        PINV[t] = 1.0 / (16.0 + PW[3, t])
        for c in range(3):
            PE[c, t] = jnp.where(PW[4 + c, t] == 1.0, PW[c, t] * PINV[t], 0.0)

    def next_plane(tiles):
        moved = [roll(v, LANES - 16, 1) for v in tiles]
        return [jnp.where(lane < LANES - 16, moved[t], moved[(t + 1) % 3]) for t in range(3)]

    def previous_plane(tiles):
        moved = [roll(v, 16, 1) for v in tiles]
        return [jnp.where(lane >= 16, moved[t], moved[(t + 2) % 3]) for t in range(3)]

    def packed_turn(colour, edges):
        ex, ey, ez = ([edges[c, t] for t in range(3)] for c in range(3))
        eyx, ezx = next_plane(ey), next_plane(ez)
        fx, fy, fz = [], [], []
        for t in range(3):
            keep = PKEEP[t]
            fx.append((ey[t] - up_lane(ey[t]) + up_row(ez[t]) - ez[t]) * keep)
            fy.append((ez[t] - ezx[t] + up_lane(ex[t]) - ex[t]) * keep)
            fz.append((ex[t] - up_row(ex[t]) + eyx[t] - ey[t]) * keep)
        fyp, fzp = previous_plane(fy), previous_plane(fz)
        for t in range(3):
            U[0, t] = jnp.where(spot == 4, ex[t], roll(fy[t], LANES - 6, 1))
            U[1, t] = jnp.where(spot == 4, ey[t], roll(fx[t], LANES - 6, 1))
            back = (
                fz[t] - down_row(fz[t]) - fy[t] + down_lane(fy[t]),
                fx[t] - down_lane(fx[t]) - fz[t] + fzp[t],
                fy[t] - fyp[t] - fx[t] + down_row(fx[t]),
            )
            for c, old in enumerate((ex[t], ey[t], ez[t])):
                residual = PW[c, t] - back[c] - PW[3, t] * old
                edges[c, t] = old + jnp.where(PW[4 + c, t] == colour + 1.0, residual * PINV[t], 0.0)

    def turn(colour, edges, packed, reach, target=None):
        packed_turn(colour, packed)

        def ends_at(xp):
            t, g = group_of(xp)
            shift = (251 - 16 * g) & (LANES - 1)
            return roll(U[0, t], shift, 1), roll(U[1, t], shift, 1)

        def moved(xp):
            ex, ey, ez = (edges[c, xp] for c in range(3))
            return ex, ey, ez, edges[1, xp + 1], edges[2, xp + 1], up_lane(ex), up_lane(ey)

        def faces(xp, values, fill):
            ex, ey, ez, ey_x, ez_x, ex_z, ey_z = values
            ex_z = jnp.where(lane == LANES - 1, fill[0], ex_z)
            ey_z = jnp.where(lane == LANES - 1, fill[1], ey_z)
            keep = low_rows * x_low(xp)
            fx = (ey - ey_z + up_row(ez) - ez) * keep
            fy = (ez - ez_x + ex_z - ex) * keep
            fz = (ex - up_row(ex) + ey_x - ey) * keep
            return fx, fy, fz

        def planes_turn(planes, carry):
            fyp, fzp = carry
            fills = [ends_at(xp) for xp in planes]
            olds = [moved(xp) for xp in planes]
            fs = [faces(xp, old, fill) for xp, old, fill in zip(planes, olds, fills)]
            backs = [(down_lane(f[0]), down_lane(f[1])) for f in fs]
            values = []
            for xp, old, fill, (fx, fy, fz), (fx_z, fy_z) in zip(planes, olds, fills, fs, backs):
                fx_z = jnp.where(lane == 0, fill[1], fx_z)
                fy_z = jnp.where(lane == 0, fill[0], fy_z)
                back = (
                    fz - down_row(fz) - fy + fy_z,
                    fx - fx_z - fz + fzp,
                    fy - fyp - fx + down_row(fx),
                )
                fyp, fzp = fy, fz
                sigma, inverse = W[3, xp], INV[xp]
                for c in range(3):
                    residual = W[c, xp] - back[c] - sigma * old[c]
                    values.append(
                        old[c] + jnp.where(W[4 + c, xp] == colour + 1.0, residual * inverse, 0.0)
                    )
            for i, xp in enumerate(planes):
                for c in range(3):
                    if target is None:
                        edges[c, xp] = values[3 * i + c]
                    else:
                        target[c, xp, OWN] = values[3 * i + c][OWN]
            return fyp, fzp

        begin = H - reach - 1
        start = faces(begin, moved(begin), ends_at(begin))
        carry = (start[1], start[2])
        every = list(range(H - reach, H + N + reach))
        for i in range(0, len(every), BATCH):
            carry = planes_turn(every[i : i + BATCH], carry)

    turn(1, E, PE, 2)
    turn(2, E, PE, 1)
    turn(3, E, PE, 0, target=E2)

    pack_own(E2, QME, 3)
    prepare(QME, XE, 3)
    copies = exchange(1, E2, QRE, XE)

    top = tab[0]
    for i in range(1, 16):
        top = jnp.maximum(top, tab[i])
    upper = jnp.full((B, LANES), 13.0 * top, jnp.float32)
    ratio = 31.0 / 29.0
    per_centre = (60.0 / 31.0) / upper
    per_half = (60.0 / 29.0) / upper

    @pl.loop(1, B, unroll=6)
    def _(xp):
        t, g = group_of(xp)
        end = roll(PW[2, t], (245 - 16 * g) & (LANES - 1), 1)
        inside = (row_mask * x_mask(xp)) > 0.0
        own = [W[c, xp] for c in range(3)]
        below = [W[0, xp - 1], down_row(own[1]), jnp.where(lane == 0, end, down_lane(own[2]))]
        values = [(below[0] - own[0]) + (below[1] - own[1]) + (below[2] - own[2])]
        values += [0.5 * (own[c] + below[c]) for c in range(3)]
        for f in range(4):
            value = jnp.where(inside, values[f], 0.0)
            NR[f, xp] = value
            value = value * per_centre
            ND[f, xp] = value
            NY[f, xp] = value

    own = [[PW[c, t] for t in range(3)] for c in range(3)]
    below = [
        previous_plane(own[0]),
        [down_row(v) for v in own[1]],
        [down_lane(v) for v in own[2]],
    ]
    for t in range(3):
        values = [sum((below[c][t] - own[c][t]) for c in range(3))]
        values += [0.5 * (own[c][t] + below[c][t]) for c in range(3)]
        for f in range(4):
            value = jnp.where(PMASK[t] > 0.0, values[f], 0.0)
            PR[f, t] = value
            value = value * per_centre
            PD[f, t] = value
            PY[f, t] = value

    rho = 1.0 / ratio
    for n in range(1, NCHEB):
        rho_next = 1.0 / (2.0 * ratio - rho)
        keep_part = rho_next * rho
        new_part = (2.0 * rho_next) * per_half
        rho = rho_next

        @pl.loop(0, 4, unroll=4)
        def _(f, keep_part=keep_part, new_part=new_part):
            mass = jnp.where(f > 0, 1.0, 0.0)
            d = [PD[f, t] for t in range(3)]
            dx = next_plane(d)
            sigma = [PW[3, t] for t in range(3)]
            wx = [sigma[t] * (dx[t] - d[t]) for t in range(3)]
            wxp = previous_plane(wx)
            for t in range(3):
                wy = sigma[t] * (up_row(d[t]) - d[t])
                wz = sigma[t] * (up_lane(d[t]) - d[t])
                UD[f, t] = jnp.where(spot == 4, d[t], roll(wz, LANES - 6, 1))
                applied = (
                    mass * sigma[t] * d[t]
                    + (wxp[t] - wx[t]) + (down_row(wy) - wy) + (down_lane(wz) - wz)
                )
                res = PR[f, t] - applied
                PR[f, t] = res
                new = jnp.where(PMASK[t] > 0.0, keep_part * d[t] + new_part * res, 0.0)
                PD[f, t] = new
                PY[f, t] = PY[f, t] + new

        low, high = n + 1, B - n

        @pl.loop(0, 4)
        def _(f, keep_part=keep_part, new_part=new_part, low=low, high=high):
            mass = jnp.where(f > 0, 1.0, 0.0)
            wxp = W[3, low - 1] * (ND[f, low] - ND[f, low - 1])
            for i in range(low, high, NBATCH):
                planes = list(range(i, min(i + NBATCH, high)))
                ends = []
                for xp in planes:
                    t, g = group_of(xp)
                    ends.append(roll(UD[f, t], (251 - 16 * g) % LANES, 1))
                ds = [ND[f, xp] for xp in planes] + [ND[f, planes[-1] + 1]]
                ups = [up_lane(d) for d in ds[:-1]]
                sigmas = [W[3, xp] for xp in planes]
                wzs = [
                    sigma * (jnp.where(lane == LANES - 1, end, up) - d)
                    for sigma, end, up, d in zip(sigmas, ends, ups, ds)
                ]
                downs = [down_lane(wz) for wz in wzs]
                for j, xp in enumerate(planes):
                    d, sigma, wz = ds[j], sigmas[j], wzs[j]
                    wx = sigma * (ds[j + 1] - d)
                    wy = sigma * (up_row(d) - d)
                    applied = (
                        (mass * sigma) * d + (wxp - wx) + (down_row(wy) - wy)
                        + (jnp.where(lane == 0, ends[j], downs[j]) - wz)
                    )
                    wxp = wx
                    res = NR[f, xp] - applied
                    inside = (row_mask * x_mask(xp)) > 0.0
                    new = jnp.where(inside, keep_part * d + new_part * res, 0.0)
                    NR[f, xp] = res
                    ND[f, xp] = new
                    NY[f, xp] = NY[f, xp] + new

        if n == 1:
            relay(1, copies, QRE, XE, 3)

    @pl.loop(0, N, unroll=4)
    def _(x):
        xp = x + H
        t, g = group_of(xp)
        shift = (251 - 16 * g) & (LANES - 1)
        potential = NY[0, xp]
        last_lane = lane == LANES - 1
        pieces = (
            (NY[0, xp + 1], NY[1, xp], NY[1, xp + 1]),
            (up_row(potential), NY[2, xp], up_row(NY[2, xp])),
            (
                jnp.where(last_lane, roll(PY[0, t], shift, 1), up_lane(potential)),
                NY[3, xp],
                jnp.where(last_lane, roll(PY[3, t], shift, 1), up_lane(NY[3, xp])),
            ),
        )
        for c, (above, own_part, next_part) in enumerate(pieces):
            out[c, x] = ((above - potential) + 0.5 * (own_part + next_part))[OWN]

    finish(copies)

    @pl.loop(0, B, unroll=4)
    def _(xp):
        inside = (row_mask * x_mask(xp)) > 0.0
        for c in range(3):
            E2[c, xp] = jnp.where(inside, E2[c, xp], 0.0)

    assemble(E2, QRE, XE, PE2, 3)
    for colour in range(4):
        turn(colour, E2, PE2, 3 - colour)

    @pl.loop(0, N, unroll=4)
    def _(x):
        for c in range(3):
            out[c, x] = out[c, x] + E2[c, x + H, OWN]


def solution(mesh):
    sizes = tuple(mesh.shape[a] for a in AXES)

    def on_device(right_side, labels, colors, table):
        f32 = jnp.float32
        plain = lambda n: pltpu.VMEM((n, B, B, LANES), f32)
        packed = lambda n: pltpu.VMEM((n, 3, B, LANES), f32)
        across = lambda k: [
            pltpu.VMEM((2, k, N, LANES), f32),
            pltpu.VMEM((2, 2, k, B, LANES), f32),
            pltpu.VMEM((len(RELAYS), k, 8, LANES), f32),
            pltpu.VMEM((2, k, B, LANES), f32),
            pltpu.VMEM((2, k, 2, N, LANES), f32),
        ]
        any_spec = pl.BlockSpec(memory_space=pltpu.HBM)
        return pl.pallas_call(
            functools.partial(kernel, sizes),
            out_shape=jax.ShapeDtypeStruct(right_side.shape, f32),
            in_specs=[any_spec] * 4,
            out_specs=pl.BlockSpec(memory_space=pltpu.VMEM),
            scratch_shapes=[
                pltpu.VMEM((3, N, N, LANES), f32),
                pltpu.VMEM((N, N, LANES), jnp.int32),
                pltpu.VMEM((3, N, N, LANES), jnp.int32),
                pltpu.SMEM((16,), f32),
                plain(7),
                pltpu.VMEM((7, 2, B, LANES), f32),
                pltpu.VMEM((2, 2, 2, B, LANES), f32),
                packed(7),
                pltpu.VMEM((B, B, LANES), f32),
                pltpu.VMEM((3, B, LANES), f32),
                pltpu.VMEM((3, B, LANES), f32),
                pltpu.VMEM((3, B, LANES), f32),
                plain(3),
                packed(3),
                plain(3),
                packed(3),
                pltpu.VMEM((3, 2, B, LANES), f32),
                pltpu.VMEM((2, 1, 2, B, LANES), f32),
                packed(2),
                plain(4),
                plain(4),
                plain(4),
                packed(4),
                packed(4),
                packed(4),
                packed(4),
                *across(2),
                *across(1),
                pltpu.SemaphoreType.DMA((4,)),
                pltpu.SemaphoreType.DMA((2, len(DIRS) + len(RELAYS))),
                pltpu.SemaphoreType.DMA((2, len(DIRS) + len(RELAYS))),
            ],
            compiler_params=pltpu.CompilerParams(
                collective_id=0, has_side_effects=True, vmem_limit_bytes=63 * 1024 * 1024
            ),
            cost_estimate=pl.CostEstimate(flops=10**8, bytes_accessed=2 * 10**6, transcendentals=0),
        )(right_side, labels, colors, table)

    in_specs = (P(None, "gx", "gy", "gz"), P("gx", "gy", "gz"), P(None, "gx", "gy", "gz"), P())
    return jax.shard_map(
        on_device, mesh=mesh, in_specs=in_specs, out_specs=P(None, "gx", "gy", "gz"), check_vma=False
    )
```

```python
import functools
import itertools

import jax
import jax.numpy as jnp
from jax import lax
from jax.experimental import pallas as pl
from jax.experimental.pallas import tpu as pltpu
from jax.sharding import PartitionSpec as P

NSWEEP = 2
NCOL = 4
NCHEB = 4
AXES = ("gx", "gy", "gz")

H = 4
N = 16
B = N + 2 * H
LANES = 128
BATCH = 5
NBATCH = 7
OWN = slice(H, H + N)
DIRS = [d for d in itertools.product((-1, 0, 1), repeat=3) if 0 < sum(map(abs, d)) < 3]
RELAYS = [(dx, dy) for dx in (-1, 1) for dy in (-1, 1)]


def roll(values, shift, axis):
    return pltpu.roll(values, shift, axis)


def down_lane(values):
    return roll(values, 1, 1)


def up_lane(values):
    return roll(values, LANES - 1, 1)


def down_row(values):
    return roll(values, 1, 0)


def up_row(values):
    return roll(values, B - 1, 0)


def group_of(xp):
    ring = (xp + (B - H)) % B if isinstance(xp, int) else jnp.where(xp >= H, xp - H, xp + (B - H))
    return ring >> 3, ring & 7


def select_table(labels, table):
    level = [table[i] for i in range(16)]
    for bit in range(4):
        odd = (labels & (1 << bit)) != 0
        level = [jnp.where(odd, level[i + 1], level[i]) for i in range(0, len(level), 2)]
    return level[0]


def kernel(
    sizes,
    r_hbm, lab_hbm, col_hbm, tab_hbm,
    out,
    r_in, lab_in, col_in, tab,
    W, QM, QR, PW, INV, PINV, PMASK, PKEEP,
    E, PE, E2, PE2, QME, QRE, U,
    NR, ND, NY, PR, PD, PY, UD,
    xs_w, xr_w, xp_w, xc_w, zs_w, xs_e, xr_e, xp_e, xc_e, zs_e,
    in_sem, ssem, rsem,
):
    XW, XE = (xs_w, xr_w, xp_w, xc_w, zs_w), (xs_e, xr_e, xp_e, xc_e, zs_e)
    here = [lax.axis_index(a) for a in AXES]
    places = [
        {
            0: here[i],
            1: jnp.where(here[i] == sizes[i] - 1, 0, here[i] + 1),
            -1: jnp.where(here[i] == 0, sizes[i] - 1, here[i] - 1),
        }
        for i in range(3)
    ]

    def neighbour(d):
        return tuple(places[i][d[i]] for i in range(3))

    def exists(d):
        found = None
        for i in range(3):
            if d[i]:
                one = here[i] < sizes[i] - 1 if d[i] > 0 else here[i] > 0
                found = one if found is None else jnp.logical_and(found, one)
        return found

    def opposite(d):
        return tuple(-step for step in d)

    loads = [
        pltpu.make_async_copy(src, dst, in_sem.at[i])
        for i, (src, dst) in enumerate(
            ((tab_hbm, tab), (lab_hbm, lab_in), (r_hbm, r_in), (col_hbm, col_in))
        )
    ]
    for load in loads:
        load.start()
    barrier = pltpu.get_barrier_semaphore()
    around = jnp.int32(0)
    for d in DIRS:
        around = around + exists(d).astype(jnp.int32)

        @pl.when(exists(d))
        def _(d=d):
            pl.semaphore_signal(
                barrier, inc=1, device_id=neighbour(d), device_id_type=pl.DeviceIdType.MESH
            )


    first = [jnp.where(here[i] > 0, 1.0, 0.0).astype(jnp.float32) for i in range(3)]
    last = [jnp.where(here[i] < sizes[i] - 1, 1.0, 0.0).astype(jnp.float32) for i in range(3)]
    lane = lax.broadcasted_iota(jnp.int32, (B, LANES), 1)
    row = lax.broadcasted_iota(jnp.int32, (B, LANES), 0)
    spot = lane % 16
    low_rows = jnp.where(row < H, first[1], 1.0)
    row_mask = low_rows * jnp.where(row >= H + N, last[1], 1.0)
    low_ends = jnp.where((spot >= 8) & (spot < 12), first[2], 1.0) * low_rows
    ends = jnp.where((spot >= 4) & (spot < 8), last[2], 1.0) * low_ends * jnp.where(
        row >= H + N, last[1], 1.0
    )
    before = jnp.where(lane >= 64, first[0], 1.0)
    after = jnp.where(lane < 64, last[0], 1.0)
    for t in range(3):
        PKEEP[t] = low_ends * before if t == 2 else low_ends
        PMASK[t] = ends * before * after if t == 2 else ends

    def x_low(xp):
        if isinstance(xp, int):
            return first[0] if xp < H else 1.0
        return jnp.where(xp >= H, 1.0, first[0])

    def x_mask(xp):
        if isinstance(xp, int):
            return last[0] if xp >= H + N else x_low(xp)
        return x_low(xp) * jnp.where(xp < H + N, 1.0, last[0])

    for load in loads:
        load.wait()

    @pl.loop(0, N, unroll=4)
    def _(x):
        W[3, x + H, OWN] = select_table(lab_in[x], tab)
        for c in range(3):
            W[c, x + H, OWN] = r_in[c, x]
            W[4 + c, x + H, OWN] = col_in[c, x].astype(jnp.float32) + 1.0

    def pack_own(src, dst, fields):
        narrow = lax.broadcasted_iota(jnp.int32, (N, LANES), 1) // 16

        @pl.loop(0, fields)
        def _(f):
            for t in range(2):
                total = None
                for g in range(8):
                    piece = roll(src[f, H + 8 * t + g, OWN], 16 * g + 4, 1)
                    total = piece if g == 0 else jnp.where(narrow == g, piece, total)
                dst[f, t, OWN] = total

    pack_own(W, QM, 7)

    def span(d, side, depth=H):
        if d == 0:
            return slice(H, H + N)
        low = (d > 0) == (side == "dst")
        if side == "dst":
            return slice(H - depth, H) if low else slice(H + N, H + N + depth)
        return slice(H, H + depth) if d < 0 else slice(H + N - depth, H + N)

    def merge(parts, half):
        shape = parts[0].shape
        lanes = lax.broadcasted_iota(jnp.int32, shape, 1)
        pair = lanes % 16 < 8
        out = jnp.where(pair, parts[0], roll(parts[1], 8, 1))
        other = roll(parts[2], 64, 1)
        if len(parts) > 3:
            other = jnp.where(pair, other, roll(parts[3], 72, 1))
        return jnp.where((lanes < 64) == (half == 0), out, other)

    def merge_quads(parts, base):
        quad = lax.broadcasted_iota(jnp.int32, parts[0].shape, 1) % 16 // 4
        out = parts[0]
        for i, part in enumerate(parts[1:], 1):
            out = jnp.where(quad == (base + i) % 4, roll(part, 4 * i, 1), out)
        return out

    def split_quad(received, side, f, t, rows):
        value = received[side, f // 4, t, rows]
        return value if f % 4 == 0 else roll(value, LANES - 4 * (f % 4), 1)

    def groups(fields):
        return [list(range(i, min(i + 4, fields))) for i in range(0, fields, 4)]

    def remote(phase, i, src, dst, d):
        return pltpu.make_async_remote_copy(
            src_ref=src,
            dst_ref=dst,
            send_sem=ssem.at[phase, i],
            recv_sem=rsem.at[phase, i],
            device_id=neighbour(d),
            device_id_type=pl.DeviceIdType.MESH,
        )

    def prepare(packed, sides, fields):
        for h in range(2):
            for k, group in enumerate(groups(fields)):
                parts = [packed[f, h, OWN] for f in group]
                sides[0][h, k] = merge(parts, h)
                for side in range(2):
                    sides[4][side, k, h] = merge_quads(parts, side)

    def exchange(phase, main, received, sides):
        sent, got = sides[0], sides[1]
        copies = {}
        for i, d in enumerate(DIRS):
            rows_src, rows_dst = span(d[1], "src"), span(d[1], "dst")
            if d[2] == 0:
                src = main.at[0:3, span(d[0], "src"), rows_src]
                dst = main.at[0:3, span(d[0], "dst"), rows_dst]
                if phase == 0:
                    copies[d + (1,)] = remote(
                        phase,
                        len(DIRS) + len(RELAYS) + i,
                        main.at[3:7, span(d[0], "src", 3), span(d[1], "src", 3)],
                        main.at[3:7, span(d[0], "dst", 3), span(d[1], "dst", 3)],
                        d,
                    )
            elif d[0] == 0:
                src = sides[4].at[0 if d[2] > 0 else 1, :, :, slice(rows_src.start - H, rows_src.stop - H)]
                dst = received.at[1 if d[2] > 0 else 0, :, :, rows_dst]
            else:
                h = 1 if d[0] > 0 else 0
                src = sent.at[h]
                dst = got.at[1 if d[2] > 0 else 0, h, :, rows_dst]
            copies[d] = remote(phase, i, src, dst, d)
        turns = [(0, 1, 1), (1, 0, 1), (1, 1, 0), (0, 1, 0), (0, 0, 1), (1, 0, 0)]
        rank = lambda d: turns.index(tuple(map(abs, d[:3])))
        for d in sorted(copies, key=rank):
            pl.when(exists(d[:3]))(copies[d].start)
        return copies

    def relay(phase, copies, received, sides, fields):
        passed, corner = sides[2], sides[3]
        for d in DIRS:
            if d[0] == 0 and d[1] and d[2]:
                pl.when(exists(opposite(d)))(copies[d].wait_recv)
        narrow = lax.broadcasted_iota(jnp.int32, (H, LANES), 1) % 16 < 4
        for i, (dx, dy) in enumerate(RELAYS):
            h, rows = (1 if dx > 0 else 0), (slice(0, H) if dy < 0 else slice(H + N, B))
            for k, group in enumerate(groups(fields)):
                parts = [
                    jnp.where(
                        narrow,
                        split_quad(received, 1, f, h, rows),
                        split_quad(received, 0, f, h, rows),
                    )
                    for f in group
                ]
                passed[i, k, 0:H] = merge(parts, h)
            copy = remote(
                phase, len(DIRS) + i, passed.at[i, :, 0:H], corner.at[h, :, rows], (dx, 0, 0)
            )
            pl.when(exists((dx, 0, 0)))(copy.start)
            copies[(dx, dy)] = copy

    def finish(copies):
        for d, copy in copies.items():
            way = d[:3] if len(d) >= 3 else (d[0], 0, 0)
            if len(d) == 2 or d[0] or not (d[1] and d[2]):
                pl.when(exists(opposite(way)))(copy.wait_recv)
            pl.when(exists(way))(copy.wait_send)

    def assemble(src, received, sides, dst, fields):
        got, corner = sides[1], sides[3]
        edge_rows = (row < H) | (row >= H + N)
        left = lane < 64
        across = [[None] * fields, [None] * fields]
        for side in range(2):
            for k, group in enumerate(groups(fields)):
                high, low = (jnp.where(edge_rows, corner[h, k], got[side, h, k]) for h in range(2))
                near, far = jnp.where(left, high, low), jnp.where(left, low, high)
                moved = (near, roll(near, 120, 1), roll(far, 64, 1), roll(far, 56, 1))
                for f, value in zip(group, moved):
                    across[side][f] = value
        for f in range(fields):
            for t in range(3):
                own = None
                for g in range(8):
                    x = (8 * t + g + H) % B
                    piece = roll(src[f, x], 16 * g + 4, 1)
                    own = piece if g == 0 else jnp.where(lane // 16 == g, piece, own)
                if t < 2:
                    high, low = (split_quad(received, side, f, t, slice(None)) for side in range(2))
                else:
                    high, low = across[0][f], across[1][f]
                upper = jnp.where(spot < 4, own, high)
                lower = roll(jnp.where(spot < 4, low, own), 8, 1)
                dst[f, t] = jnp.where(PMASK[t] > 0.0, jnp.where(spot < 8, upper, lower), 0.0)

    prepare(QM, XW, 7)
    pl.semaphore_wait(barrier, around)
    copies = exchange(0, W, QR, XW)
    relay(0, copies, QR, XW, 7)
    finish(copies)

    @pl.loop(0, B, unroll=4)
    def _(xp):
        inside = (row_mask * x_mask(xp)) > 0.0
        for f in range(7):
            W[f, xp] = jnp.where(inside, W[f, xp], 0.0)
        inverse = 1.0 / (16.0 + W[3, xp])
        INV[xp] = inverse
        for c in range(3):
            E[c, xp] = jnp.where(W[4 + c, xp] == 1.0, W[c, xp] * inverse, 0.0)

    assemble(W, QR, XW, PW, 7)
    for t in range(3):
        PINV[t] = 1.0 / (16.0 + PW[3, t])
        for c in range(3):
            PE[c, t] = jnp.where(PW[4 + c, t] == 1.0, PW[c, t] * PINV[t], 0.0)

    def next_plane(tiles):
        moved = [roll(v, LANES - 16, 1) for v in tiles]
        return [jnp.where(lane < LANES - 16, moved[t], moved[(t + 1) % 3]) for t in range(3)]

    def previous_plane(tiles):
        moved = [roll(v, 16, 1) for v in tiles]
        return [jnp.where(lane >= 16, moved[t], moved[(t + 2) % 3]) for t in range(3)]

    def packed_turn(colour, edges):
        ex, ey, ez = ([edges[c, t] for t in range(3)] for c in range(3))
        eyx, ezx = next_plane(ey), next_plane(ez)
        fx, fy, fz = [], [], []
        for t in range(3):
            keep = PKEEP[t]
            fx.append((ey[t] - up_lane(ey[t]) + up_row(ez[t]) - ez[t]) * keep)
            fy.append((ez[t] - ezx[t] + up_lane(ex[t]) - ex[t]) * keep)
            fz.append((ex[t] - up_row(ex[t]) + eyx[t] - ey[t]) * keep)
        fyp, fzp = previous_plane(fy), previous_plane(fz)
        for t in range(3):
            U[0, t] = jnp.where(spot == 4, ex[t], roll(fy[t], LANES - 6, 1))
            U[1, t] = jnp.where(spot == 4, ey[t], roll(fx[t], LANES - 6, 1))
            back = (
                fz[t] - down_row(fz[t]) - fy[t] + down_lane(fy[t]),
                fx[t] - down_lane(fx[t]) - fz[t] + fzp[t],
                fy[t] - fyp[t] - fx[t] + down_row(fx[t]),
            )
            for c, old in enumerate((ex[t], ey[t], ez[t])):
                residual = PW[c, t] - back[c] - PW[3, t] * old
                edges[c, t] = old + jnp.where(PW[4 + c, t] == colour + 1.0, residual * PINV[t], 0.0)

    def turn(colour, edges, packed, reach, target=None):
        packed_turn(colour, packed)

        def ends_at(xp):
            t, g = group_of(xp)
            shift = (251 - 16 * g) & (LANES - 1)
            return roll(U[0, t], shift, 1), roll(U[1, t], shift, 1)

        def moved(xp):
            ex, ey, ez = (edges[c, xp] for c in range(3))
            return ex, ey, ez, edges[1, xp + 1], edges[2, xp + 1], up_lane(ex), up_lane(ey)

        def faces(xp, values, fill):
            ex, ey, ez, ey_x, ez_x, ex_z, ey_z = values
            ex_z = jnp.where(lane == LANES - 1, fill[0], ex_z)
            ey_z = jnp.where(lane == LANES - 1, fill[1], ey_z)
            keep = low_rows * x_low(xp)
            fx = (ey - ey_z + up_row(ez) - ez) * keep
            fy = (ez - ez_x + ex_z - ex) * keep
            fz = (ex - up_row(ex) + ey_x - ey) * keep
            return fx, fy, fz

        def planes_turn(planes, carry):
            fyp, fzp = carry
            fills = [ends_at(xp) for xp in planes]
            olds = [moved(xp) for xp in planes]
            fs = [faces(xp, old, fill) for xp, old, fill in zip(planes, olds, fills)]
            backs = [(down_lane(f[0]), down_lane(f[1])) for f in fs]
            values = []
            for xp, old, fill, (fx, fy, fz), (fx_z, fy_z) in zip(planes, olds, fills, fs, backs):
                fx_z = jnp.where(lane == 0, fill[1], fx_z)
                fy_z = jnp.where(lane == 0, fill[0], fy_z)
                back = (
                    fz - down_row(fz) - fy + fy_z,
                    fx - fx_z - fz + fzp,
                    fy - fyp - fx + down_row(fx),
                )
                fyp, fzp = fy, fz
                sigma, inverse = W[3, xp], INV[xp]
                for c in range(3):
                    residual = W[c, xp] - back[c] - sigma * old[c]
                    values.append(
                        old[c] + jnp.where(W[4 + c, xp] == colour + 1.0, residual * inverse, 0.0)
                    )
            for i, xp in enumerate(planes):
                for c in range(3):
                    if target is None:
                        edges[c, xp] = values[3 * i + c]
                    else:
                        target[c, xp, OWN] = values[3 * i + c][OWN]
            return fyp, fzp

        begin = H - reach - 1
        start = faces(begin, moved(begin), ends_at(begin))
        carry = (start[1], start[2])
        every = list(range(H - reach, H + N + reach))
        for i in range(0, len(every), BATCH):
            carry = planes_turn(every[i : i + BATCH], carry)

    turn(1, E, PE, 2)
    turn(2, E, PE, 1)
    turn(3, E, PE, 0, target=E2)

    pack_own(E2, QME, 3)
    prepare(QME, XE, 3)
    copies = exchange(1, E2, QRE, XE)

    top = tab[0]
    for i in range(1, 16):
        top = jnp.maximum(top, tab[i])
    upper = jnp.full((B, LANES), 13.0 * top, jnp.float32)
    ratio = 31.0 / 29.0
    per_centre = (60.0 / 31.0) / upper
    per_half = (60.0 / 29.0) / upper

    @pl.loop(1, B, unroll=6)
    def _(xp):
        t, g = group_of(xp)
        end = roll(PW[2, t], (245 - 16 * g) & (LANES - 1), 1)
        inside = (row_mask * x_mask(xp)) > 0.0
        own = [W[c, xp] for c in range(3)]
        below = [W[0, xp - 1], down_row(own[1]), jnp.where(lane == 0, end, down_lane(own[2]))]
        values = [(below[0] - own[0]) + (below[1] - own[1]) + (below[2] - own[2])]
        values += [0.5 * (own[c] + below[c]) for c in range(3)]
        for f in range(4):
            value = jnp.where(inside, values[f], 0.0)
            NR[f, xp] = value
            value = value * per_centre
            ND[f, xp] = value
            NY[f, xp] = value

    own = [[PW[c, t] for t in range(3)] for c in range(3)]
    below = [
        previous_plane(own[0]),
        [down_row(v) for v in own[1]],
        [down_lane(v) for v in own[2]],
    ]
    for t in range(3):
        values = [sum((below[c][t] - own[c][t]) for c in range(3))]
        values += [0.5 * (own[c][t] + below[c][t]) for c in range(3)]
        for f in range(4):
            value = jnp.where(PMASK[t] > 0.0, values[f], 0.0)
            PR[f, t] = value
            value = value * per_centre
            PD[f, t] = value
            PY[f, t] = value

    rho = 1.0 / ratio
    for n in range(1, NCHEB):
        rho_next = 1.0 / (2.0 * ratio - rho)
        keep_part = rho_next * rho
        new_part = (2.0 * rho_next) * per_half
        rho = rho_next

        @pl.loop(0, 4, unroll=4)
        def _(f, keep_part=keep_part, new_part=new_part):
            mass = jnp.where(f > 0, 1.0, 0.0)
            d = [PD[f, t] for t in range(3)]
            dx = next_plane(d)
            sigma = [PW[3, t] for t in range(3)]
            wx = [sigma[t] * (dx[t] - d[t]) for t in range(3)]
            wxp = previous_plane(wx)
            for t in range(3):
                wy = sigma[t] * (up_row(d[t]) - d[t])
                wz = sigma[t] * (up_lane(d[t]) - d[t])
                UD[f, t] = jnp.where(spot == 4, d[t], roll(wz, LANES - 6, 1))
                applied = (
                    mass * sigma[t] * d[t]
                    + (wxp[t] - wx[t]) + (down_row(wy) - wy) + (down_lane(wz) - wz)
                )
                res = PR[f, t] - applied
                PR[f, t] = res
                new = jnp.where(PMASK[t] > 0.0, keep_part * d[t] + new_part * res, 0.0)
                PD[f, t] = new
                PY[f, t] = PY[f, t] + new

        low, high = n + 1, B - n

        @pl.loop(0, 4)
        def _(f, keep_part=keep_part, new_part=new_part, low=low, high=high):
            mass = jnp.where(f > 0, 1.0, 0.0)
            wxp = W[3, low - 1] * (ND[f, low] - ND[f, low - 1])
            for i in range(low, high, NBATCH):
                planes = list(range(i, min(i + NBATCH, high)))
                ends = []
                for xp in planes:
                    t, g = group_of(xp)
                    ends.append(roll(UD[f, t], (251 - 16 * g) % LANES, 1))
                ds = [ND[f, xp] for xp in planes] + [ND[f, planes[-1] + 1]]
                ups = [up_lane(d) for d in ds[:-1]]
                sigmas = [W[3, xp] for xp in planes]
                wzs = [
                    sigma * (jnp.where(lane == LANES - 1, end, up) - d)
                    for sigma, end, up, d in zip(sigmas, ends, ups, ds)
                ]
                downs = [down_lane(wz) for wz in wzs]
                for j, xp in enumerate(planes):
                    d, sigma, wz = ds[j], sigmas[j], wzs[j]
                    wx = sigma * (ds[j + 1] - d)
                    wy = sigma * (up_row(d) - d)
                    applied = (
                        (mass * sigma) * d + (wxp - wx) + (down_row(wy) - wy)
                        + (jnp.where(lane == 0, ends[j], downs[j]) - wz)
                    )
                    wxp = wx
                    res = NR[f, xp] - applied
                    inside = (row_mask * x_mask(xp)) > 0.0
                    new = jnp.where(inside, keep_part * d + new_part * res, 0.0)
                    NR[f, xp] = res
                    ND[f, xp] = new
                    NY[f, xp] = NY[f, xp] + new

        if n == 1:
            relay(1, copies, QRE, XE, 3)

    @pl.loop(0, N, unroll=4)
    def _(x):
        xp = x + H
        t, g = group_of(xp)
        shift = (251 - 16 * g) & (LANES - 1)
        potential = NY[0, xp]
        last_lane = lane == LANES - 1
        pieces = (
            (NY[0, xp + 1], NY[1, xp], NY[1, xp + 1]),
            (up_row(potential), NY[2, xp], up_row(NY[2, xp])),
            (
                jnp.where(last_lane, roll(PY[0, t], shift, 1), up_lane(potential)),
                NY[3, xp],
                jnp.where(last_lane, roll(PY[3, t], shift, 1), up_lane(NY[3, xp])),
            ),
        )
        for c, (above, own_part, next_part) in enumerate(pieces):
            out[c, x] = ((above - potential) + 0.5 * (own_part + next_part))[OWN]

    finish(copies)

    @pl.loop(0, B, unroll=4)
    def _(xp):
        inside = (row_mask * x_mask(xp)) > 0.0
        for c in range(3):
            E2[c, xp] = jnp.where(inside, E2[c, xp], 0.0)

    assemble(E2, QRE, XE, PE2, 3)
    for colour in range(4):
        turn(colour, E2, PE2, 3 - colour)

    @pl.loop(0, N, unroll=4)
    def _(x):
        for c in range(3):
            out[c, x] = out[c, x] + E2[c, x + H, OWN]


def solution(mesh):
    sizes = tuple(mesh.shape[a] for a in AXES)

    def on_device(right_side, labels, colors, table):
        f32 = jnp.float32
        plain = lambda n: pltpu.VMEM((n, B, B, LANES), f32)
        packed = lambda n: pltpu.VMEM((n, 3, B, LANES), f32)
        across = lambda k: [
            pltpu.VMEM((2, k, N, LANES), f32),
            pltpu.VMEM((2, 2, k, B, LANES), f32),
            pltpu.VMEM((len(RELAYS), k, 8, LANES), f32),
            pltpu.VMEM((2, k, B, LANES), f32),
            pltpu.VMEM((2, k, 2, N, LANES), f32),
        ]
        any_spec = pl.BlockSpec(memory_space=pltpu.HBM)
        return pl.pallas_call(
            functools.partial(kernel, sizes),
            out_shape=jax.ShapeDtypeStruct(right_side.shape, f32),
            in_specs=[any_spec] * 4,
            out_specs=pl.BlockSpec(memory_space=pltpu.VMEM),
            scratch_shapes=[
                pltpu.VMEM((3, N, N, LANES), f32),
                pltpu.VMEM((N, N, LANES), jnp.int32),
                pltpu.VMEM((3, N, N, LANES), jnp.int32),
                pltpu.SMEM((16,), f32),
                plain(7),
                pltpu.VMEM((7, 2, B, LANES), f32),
                pltpu.VMEM((2, 2, 2, B, LANES), f32),
                packed(7),
                pltpu.VMEM((B, B, LANES), f32),
                pltpu.VMEM((3, B, LANES), f32),
                pltpu.VMEM((3, B, LANES), f32),
                pltpu.VMEM((3, B, LANES), f32),
                plain(3),
                packed(3),
                plain(3),
                packed(3),
                pltpu.VMEM((3, 2, B, LANES), f32),
                pltpu.VMEM((2, 1, 2, B, LANES), f32),
                packed(2),
                plain(4),
                plain(4),
                plain(4),
                packed(4),
                packed(4),
                packed(4),
                packed(4),
                *across(2),
                *across(1),
                pltpu.SemaphoreType.DMA((4,)),
                pltpu.SemaphoreType.DMA((2, 2 * len(DIRS) + len(RELAYS))),
                pltpu.SemaphoreType.DMA((2, 2 * len(DIRS) + len(RELAYS))),
            ],
            compiler_params=pltpu.CompilerParams(
                collective_id=0, has_side_effects=True, vmem_limit_bytes=63 * 1024 * 1024
            ),
            cost_estimate=pl.CostEstimate(flops=10**8, bytes_accessed=2 * 10**6, transcendentals=0),
        )(right_side, labels, colors, table)

    in_specs = (P(None, "gx", "gy", "gz"), P("gx", "gy", "gz"), P(None, "gx", "gy", "gz"), P())
    return jax.shard_map(
        on_device, mesh=mesh, in_specs=in_specs, out_specs=P(None, "gx", "gy", "gz"), check_vma=False
    )
```

```python
import functools
import itertools

import jax
import jax.numpy as jnp
from jax import lax
from jax.experimental import pallas as pl
from jax.experimental.pallas import tpu as pltpu
from jax.sharding import PartitionSpec as P

NSWEEP = 2
NCOL = 4
NCHEB = 4
AXES = ("gx", "gy", "gz")

H = 4
N = 16
B = N + 2 * H
LANES = 128
BATCH = 5
NBATCH = 7
OWN = slice(H, H + N)
DIRS = [d for d in itertools.product((-1, 0, 1), repeat=3) if 0 < sum(map(abs, d)) < 3]
RELAYS = [(dx, dy) for dx in (-1, 1) for dy in (-1, 1)]


def roll(values, shift, axis):
    return pltpu.roll(values, shift, axis)


def down_lane(values):
    return roll(values, 1, 1)


def up_lane(values):
    return roll(values, LANES - 1, 1)


def down_row(values):
    return roll(values, 1, 0)


def up_row(values):
    return roll(values, B - 1, 0)


def group_of(xp):
    ring = (xp + (B - H)) % B if isinstance(xp, int) else jnp.where(xp >= H, xp - H, xp + (B - H))
    return ring >> 3, ring & 7


def select_table(labels, table):
    level = [table[i] for i in range(16)]
    for bit in range(4):
        odd = (labels & (1 << bit)) != 0
        level = [jnp.where(odd, level[i + 1], level[i]) for i in range(0, len(level), 2)]
    return level[0]


def kernel(
    sizes,
    r_hbm, lab_hbm, col_hbm, tab_hbm,
    out,
    r_in, lab_in, col_in, tab,
    W, QM, QR, PW, INV, PINV, PMASK, PKEEP,
    E, PE, E2, PE2, QME, QRE, U,
    NR, ND, NY, PR, PD, PY, UD,
    xs_w, xr_w, xp_w, xc_w, zs_w, xs_e, xr_e, xp_e, xc_e, zs_e,
    in_sem, ssem, rsem,
):
    XW, XE = (xs_w, xr_w, xp_w, xc_w, zs_w), (xs_e, xr_e, xp_e, xc_e, zs_e)
    here = [lax.axis_index(a) for a in AXES]
    places = [
        {
            0: here[i],
            1: jnp.where(here[i] == sizes[i] - 1, 0, here[i] + 1),
            -1: jnp.where(here[i] == 0, sizes[i] - 1, here[i] - 1),
        }
        for i in range(3)
    ]

    def neighbour(d):
        return tuple(places[i][d[i]] for i in range(3))

    def exists(d):
        found = None
        for i in range(3):
            if d[i]:
                one = here[i] < sizes[i] - 1 if d[i] > 0 else here[i] > 0
                found = one if found is None else jnp.logical_and(found, one)
        return found

    def opposite(d):
        return tuple(-step for step in d)

    loads = [
        pltpu.make_async_copy(src, dst, in_sem.at[i])
        for i, (src, dst) in enumerate(
            ((tab_hbm, tab), (lab_hbm, lab_in), (r_hbm, r_in), (col_hbm, col_in))
        )
    ]
    for load in loads:
        load.start()
    barrier = pltpu.get_barrier_semaphore()
    around = jnp.int32(0)
    for d in DIRS:
        around = around + exists(d).astype(jnp.int32)

        @pl.when(exists(d))
        def _(d=d):
            pl.semaphore_signal(
                barrier, inc=1, device_id=neighbour(d), device_id_type=pl.DeviceIdType.MESH
            )


    first = [jnp.where(here[i] > 0, 1.0, 0.0).astype(jnp.float32) for i in range(3)]
    last = [jnp.where(here[i] < sizes[i] - 1, 1.0, 0.0).astype(jnp.float32) for i in range(3)]
    lane = lax.broadcasted_iota(jnp.int32, (B, LANES), 1)
    row = lax.broadcasted_iota(jnp.int32, (B, LANES), 0)
    spot = lane % 16
    low_rows = jnp.where(row < H, first[1], 1.0)
    row_mask = low_rows * jnp.where(row >= H + N, last[1], 1.0)
    low_ends = jnp.where((spot >= 8) & (spot < 12), first[2], 1.0) * low_rows
    ends = jnp.where((spot >= 4) & (spot < 8), last[2], 1.0) * low_ends * jnp.where(
        row >= H + N, last[1], 1.0
    )
    before = jnp.where(lane >= 64, first[0], 1.0)
    after = jnp.where(lane < 64, last[0], 1.0)
    for t in range(3):
        PKEEP[t] = low_ends * before if t == 2 else low_ends
        PMASK[t] = ends * before * after if t == 2 else ends

    def x_low(xp):
        if isinstance(xp, int):
            return first[0] if xp < H else 1.0
        return jnp.where(xp >= H, 1.0, first[0])

    def x_mask(xp):
        if isinstance(xp, int):
            return last[0] if xp >= H + N else x_low(xp)
        return x_low(xp) * jnp.where(xp < H + N, 1.0, last[0])

    for load in loads:
        load.wait()

    @pl.loop(0, N, unroll=4)
    def _(x):
        W[3, x + H, OWN] = select_table(lab_in[x], tab)
        for c in range(3):
            W[c, x + H, OWN] = r_in[c, x]
            W[4 + c, x + H, OWN] = col_in[c, x].astype(jnp.float32) + 1.0

    def pack_own(src, dst, fields):
        narrow = lax.broadcasted_iota(jnp.int32, (N, LANES), 1) // 16

        @pl.loop(0, fields)
        def _(f):
            for t in range(2):
                total = None
                for g in range(8):
                    piece = roll(src[f, H + 8 * t + g, OWN], 16 * g + 4, 1)
                    total = piece if g == 0 else jnp.where(narrow == g, piece, total)
                dst[f, t, OWN] = total

    pack_own(W, QM, 7)

    def span(d, side, depth=H):
        if d == 0:
            return slice(H, H + N)
        low = (d > 0) == (side == "dst")
        if side == "dst":
            return slice(H - depth, H) if low else slice(H + N, H + N + depth)
        return slice(H, H + depth) if d < 0 else slice(H + N - depth, H + N)

    def merge(parts, half):
        shape = parts[0].shape
        lanes = lax.broadcasted_iota(jnp.int32, shape, 1)
        pair = lanes % 16 < 8
        out = jnp.where(pair, parts[0], roll(parts[1], 8, 1))
        other = roll(parts[2], 64, 1)
        if len(parts) > 3:
            other = jnp.where(pair, other, roll(parts[3], 72, 1))
        return jnp.where((lanes < 64) == (half == 0), out, other)

    def merge_quads(parts, base):
        quad = lax.broadcasted_iota(jnp.int32, parts[0].shape, 1) % 16 // 4
        out = parts[0]
        for i, part in enumerate(parts[1:], 1):
            out = jnp.where(quad == (base + i) % 4, roll(part, 4 * i, 1), out)
        return out

    def split_quad(received, side, f, t, rows):
        value = received[side, f // 4, t, rows]
        return value if f % 4 == 0 else roll(value, LANES - 4 * (f % 4), 1)

    def groups(fields):
        return [list(range(i, min(i + 4, fields))) for i in range(0, fields, 4)]

    def remote(phase, i, src, dst, d):
        return pltpu.make_async_remote_copy(
            src_ref=src,
            dst_ref=dst,
            send_sem=ssem.at[phase, i],
            recv_sem=rsem.at[phase, i],
            device_id=neighbour(d),
            device_id_type=pl.DeviceIdType.MESH,
        )

    def prepare(packed, sides, fields):
        for h in range(2):
            for k, group in enumerate(groups(fields)):
                parts = [packed[f, h, OWN] for f in group]
                sides[0][h, k] = merge(parts, h)
                for side in range(2):
                    sides[4][side, k, h] = merge_quads(parts, side)

    def exchange(phase, main, received, sides):
        sent, got = sides[0], sides[1]
        copies = {}
        for i, d in enumerate(DIRS):
            rows_src, rows_dst = span(d[1], "src"), span(d[1], "dst")
            if d[2] == 0:
                src = main.at[0:3, span(d[0], "src"), rows_src]
                dst = main.at[0:3, span(d[0], "dst"), rows_dst]
                if phase == 0:
                    copies[d + (1,)] = remote(
                        phase,
                        len(DIRS) + len(RELAYS) + i,
                        main.at[3:7, span(d[0], "src", 3), span(d[1], "src", 3)],
                        main.at[3:7, span(d[0], "dst", 3), span(d[1], "dst", 3)],
                        d,
                    )
            elif d[0] == 0:
                src = sides[4].at[0 if d[2] > 0 else 1, :, :, slice(rows_src.start - H, rows_src.stop - H)]
                dst = received.at[1 if d[2] > 0 else 0, :, :, rows_dst]
            else:
                h = 1 if d[0] > 0 else 0
                src = sent.at[h]
                dst = got.at[1 if d[2] > 0 else 0, h, :, rows_dst]
            copies[d] = remote(phase, i, src, dst, d)
        turns = [(0, 1, 1), (1, 0, 1), (1, 1, 0), (0, 1, 0), (0, 0, 1), (1, 0, 0)]
        rank = lambda d: turns.index(tuple(map(abs, d[:3])))
        for d in sorted(copies, key=rank):
            pl.when(exists(d[:3]))(copies[d].start)
        return copies

    def relay(phase, copies, received, sides, fields):
        passed, corner = sides[2], sides[3]
        for d in DIRS:
            if d[0] == 0 and d[1] and d[2]:
                pl.when(exists(opposite(d)))(copies[d].wait_recv)
        narrow = lax.broadcasted_iota(jnp.int32, (H, LANES), 1) % 16 < 4
        for i, (dx, dy) in enumerate(RELAYS):
            h, rows = (1 if dx > 0 else 0), (slice(0, H) if dy < 0 else slice(H + N, B))
            for k, group in enumerate(groups(fields)):
                parts = [
                    jnp.where(
                        narrow,
                        split_quad(received, 1, f, h, rows),
                        split_quad(received, 0, f, h, rows),
                    )
                    for f in group
                ]
                passed[i, k, 0:H] = merge(parts, h)
            copy = remote(
                phase, len(DIRS) + i, passed.at[i, :, 0:H], corner.at[h, :, rows], (dx, 0, 0)
            )
            pl.when(exists((dx, 0, 0)))(copy.start)
            copies[(dx, dy)] = copy

    def finish(copies):
        for d, copy in copies.items():
            way = d[:3] if len(d) >= 3 else (d[0], 0, 0)
            if len(d) == 2 or d[0] or not (d[1] and d[2]):
                pl.when(exists(opposite(way)))(copy.wait_recv)
            pl.when(exists(way))(copy.wait_send)

    def assemble(src, received, sides, dst, fields):
        got, corner = sides[1], sides[3]
        edge_rows = (row < H) | (row >= H + N)
        left = lane < 64
        across = [[None] * fields, [None] * fields]
        for side in range(2):
            for k, group in enumerate(groups(fields)):
                high, low = (jnp.where(edge_rows, corner[h, k], got[side, h, k]) for h in range(2))
                near, far = jnp.where(left, high, low), jnp.where(left, low, high)
                moved = (near, roll(near, 120, 1), roll(far, 64, 1), roll(far, 56, 1))
                for f, value in zip(group, moved):
                    across[side][f] = value
        for f in range(fields):
            for t in range(3):
                own = None
                for g in range(8):
                    x = (8 * t + g + H) % B
                    piece = roll(src[f, x], 16 * g + 4, 1)
                    own = piece if g == 0 else jnp.where(lane // 16 == g, piece, own)
                if t < 2:
                    high, low = (split_quad(received, side, f, t, slice(None)) for side in range(2))
                else:
                    high, low = across[0][f], across[1][f]
                upper = jnp.where(spot < 4, own, high)
                lower = roll(jnp.where(spot < 4, low, own), 8, 1)
                dst[f, t] = jnp.where(PMASK[t] > 0.0, jnp.where(spot < 8, upper, lower), 0.0)

    prepare(QM, XW, 7)
    pl.semaphore_wait(barrier, around)
    copies = exchange(0, W, QR, XW)
    relay(0, copies, QR, XW, 7)
    finish(copies)

    @pl.loop(0, B, unroll=4)
    def _(xp):
        inside = (row_mask * x_mask(xp)) > 0.0
        for f in range(7):
            W[f, xp] = jnp.where(inside, W[f, xp], 0.0)
        inverse = 1.0 / (16.0 + W[3, xp])
        INV[xp] = inverse
        for c in range(3):
            E[c, xp] = jnp.where(W[4 + c, xp] == 1.0, W[c, xp] * inverse, 0.0)

    assemble(W, QR, XW, PW, 7)
    for t in range(3):
        PINV[t] = 1.0 / (16.0 + PW[3, t])
        for c in range(3):
            PE[c, t] = jnp.where(PW[4 + c, t] == 1.0, PW[c, t] * PINV[t], 0.0)

    def next_plane(tiles):
        moved = [roll(v, LANES - 16, 1) for v in tiles]
        return [jnp.where(lane < LANES - 16, moved[t], moved[(t + 1) % 3]) for t in range(3)]

    def previous_plane(tiles):
        moved = [roll(v, 16, 1) for v in tiles]
        return [jnp.where(lane >= 16, moved[t], moved[(t + 2) % 3]) for t in range(3)]

    def packed_turn(colour, edges):
        ex, ey, ez = ([edges[c, t] for t in range(3)] for c in range(3))
        eyx, ezx = next_plane(ey), next_plane(ez)
        fx, fy, fz = [], [], []
        for t in range(3):
            keep = PKEEP[t]
            fx.append((ey[t] - up_lane(ey[t]) + up_row(ez[t]) - ez[t]) * keep)
            fy.append((ez[t] - ezx[t] + up_lane(ex[t]) - ex[t]) * keep)
            fz.append((ex[t] - up_row(ex[t]) + eyx[t] - ey[t]) * keep)
        fyp, fzp = previous_plane(fy), previous_plane(fz)
        for t in range(3):
            U[0, t] = jnp.where(spot == 4, ex[t], roll(fy[t], LANES - 6, 1))
            U[1, t] = jnp.where(spot == 4, ey[t], roll(fx[t], LANES - 6, 1))
            back = (
                fz[t] - down_row(fz[t]) - fy[t] + down_lane(fy[t]),
                fx[t] - down_lane(fx[t]) - fz[t] + fzp[t],
                fy[t] - fyp[t] - fx[t] + down_row(fx[t]),
            )
            for c, old in enumerate((ex[t], ey[t], ez[t])):
                residual = PW[c, t] - back[c] - PW[3, t] * old
                edges[c, t] = old + jnp.where(PW[4 + c, t] == colour + 1.0, residual * PINV[t], 0.0)

    def turn(colour, edges, packed, reach, target=None):
        packed_turn(colour, packed)

        def ends_at(xp):
            t, g = group_of(xp)
            shift = (251 - 16 * g) & (LANES - 1)
            return roll(U[0, t], shift, 1), roll(U[1, t], shift, 1)

        def moved(xp):
            ex, ey, ez = (edges[c, xp] for c in range(3))
            return ex, ey, ez, edges[1, xp + 1], edges[2, xp + 1], up_lane(ex), up_lane(ey)

        def faces(xp, values, fill):
            ex, ey, ez, ey_x, ez_x, ex_z, ey_z = values
            ex_z = jnp.where(lane == LANES - 1, fill[0], ex_z)
            ey_z = jnp.where(lane == LANES - 1, fill[1], ey_z)
            keep = low_rows * x_low(xp)
            fx = (ey - ey_z + up_row(ez) - ez) * keep
            fy = (ez - ez_x + ex_z - ex) * keep
            fz = (ex - up_row(ex) + ey_x - ey) * keep
            return fx, fy, fz

        def planes_turn(planes, carry):
            fyp, fzp = carry
            fills = [ends_at(xp) for xp in planes]
            olds = [moved(xp) for xp in planes]
            fs = [faces(xp, old, fill) for xp, old, fill in zip(planes, olds, fills)]
            backs = [(down_lane(f[0]), down_lane(f[1])) for f in fs]
            values = []
            for xp, old, fill, (fx, fy, fz), (fx_z, fy_z) in zip(planes, olds, fills, fs, backs):
                fx_z = jnp.where(lane == 0, fill[1], fx_z)
                fy_z = jnp.where(lane == 0, fill[0], fy_z)
                back = (
                    fz - down_row(fz) - fy + fy_z,
                    fx - fx_z - fz + fzp,
                    fy - fyp - fx + down_row(fx),
                )
                fyp, fzp = fy, fz
                sigma, inverse = W[3, xp], INV[xp]
                for c in range(3):
                    residual = W[c, xp] - back[c] - sigma * old[c]
                    values.append(
                        old[c] + jnp.where(W[4 + c, xp] == colour + 1.0, residual * inverse, 0.0)
                    )
            for i, xp in enumerate(planes):
                for c in range(3):
                    if target is None:
                        edges[c, xp] = values[3 * i + c]
                    else:
                        target[c, xp, OWN] = values[3 * i + c][OWN]
            return fyp, fzp

        begin = H - reach - 1
        start = faces(begin, moved(begin), ends_at(begin))
        carry = (start[1], start[2])
        every = list(range(H - reach, H + N + reach))
        for i in range(0, len(every), BATCH):
            carry = planes_turn(every[i : i + BATCH], carry)

    turn(1, E, PE, 2)
    turn(2, E, PE, 1)
    turn(3, E, PE, 0, target=E2)

    pack_own(E2, QME, 3)
    prepare(QME, XE, 3)
    copies = exchange(1, E2, QRE, XE)

    top = tab[0]
    for i in range(1, 16):
        top = jnp.maximum(top, tab[i])
    upper = jnp.full((B, LANES), 13.0 * top, jnp.float32)
    ratio = 31.0 / 29.0
    per_centre = (60.0 / 31.0) / upper
    per_half = (60.0 / 29.0) / upper

    @pl.loop(1, B, unroll=6)
    def _(xp):
        t, g = group_of(xp)
        end = roll(PW[2, t], (245 - 16 * g) & (LANES - 1), 1)
        inside = (row_mask * x_mask(xp)) > 0.0
        own = [W[c, xp] for c in range(3)]
        below = [W[0, xp - 1], down_row(own[1]), jnp.where(lane == 0, end, down_lane(own[2]))]
        values = [(below[0] - own[0]) + (below[1] - own[1]) + (below[2] - own[2])]
        values += [0.5 * (own[c] + below[c]) for c in range(3)]
        for f in range(4):
            value = jnp.where(inside, values[f], 0.0)
            NR[f, xp] = value
            value = value * per_centre
            ND[f, xp] = value
            NY[f, xp] = value

    own = [[PW[c, t] for t in range(3)] for c in range(3)]
    below = [
        previous_plane(own[0]),
        [down_row(v) for v in own[1]],
        [down_lane(v) for v in own[2]],
    ]
    for t in range(3):
        values = [sum((below[c][t] - own[c][t]) for c in range(3))]
        values += [0.5 * (own[c][t] + below[c][t]) for c in range(3)]
        for f in range(4):
            value = jnp.where(PMASK[t] > 0.0, values[f], 0.0)
            PR[f, t] = value
            value = value * per_centre
            PD[f, t] = value
            PY[f, t] = value

    rho = 1.0 / ratio
    for n in range(1, NCHEB):
        rho_next = 1.0 / (2.0 * ratio - rho)
        keep_part = rho_next * rho
        new_part = (2.0 * rho_next) * per_half
        rho = rho_next

        @pl.loop(0, 4, unroll=4)
        def _(f, keep_part=keep_part, new_part=new_part):
            mass = jnp.where(f > 0, 1.0, 0.0)
            d = [PD[f, t] for t in range(3)]
            dx = next_plane(d)
            sigma = [PW[3, t] for t in range(3)]
            wx = [sigma[t] * (dx[t] - d[t]) for t in range(3)]
            wxp = previous_plane(wx)
            for t in range(3):
                wy = sigma[t] * (up_row(d[t]) - d[t])
                wz = sigma[t] * (up_lane(d[t]) - d[t])
                UD[f, t] = jnp.where(spot == 4, d[t], roll(wz, LANES - 6, 1))
                applied = (
                    mass * sigma[t] * d[t]
                    + (wxp[t] - wx[t]) + (down_row(wy) - wy) + (down_lane(wz) - wz)
                )
                res = PR[f, t] - applied
                PR[f, t] = res
                new = jnp.where(PMASK[t] > 0.0, keep_part * d[t] + new_part * res, 0.0)
                PD[f, t] = new
                PY[f, t] = PY[f, t] + new

        low, high = n + 1, B - n

        @pl.loop(0, 4, unroll=2)
        def _(f, keep_part=keep_part, new_part=new_part, low=low, high=high, more=n + 1 < NCHEB):
            mass = jnp.where(f > 0, 1.0, 0.0)
            wxp = W[3, low - 1] * (ND[f, low] - ND[f, low - 1])
            for i in range(low, high, NBATCH):
                planes = list(range(i, min(i + NBATCH, high)))
                ends = []
                for xp in planes:
                    t, g = group_of(xp)
                    ends.append(roll(UD[f, t], (251 - 16 * g) % LANES, 1))
                ds = [ND[f, xp] for xp in planes] + [ND[f, planes[-1] + 1]]
                ups = [up_lane(d) for d in ds[:-1]]
                sigmas = [W[3, xp] for xp in planes]
                wzs = [
                    sigma * (jnp.where(lane == LANES - 1, end, up) - d)
                    for sigma, end, up, d in zip(sigmas, ends, ups, ds)
                ]
                downs = [down_lane(wz) for wz in wzs]
                for j, xp in enumerate(planes):
                    d, sigma, wz = ds[j], sigmas[j], wzs[j]
                    wx = sigma * (ds[j + 1] - d)
                    wy = sigma * (up_row(d) - d)
                    applied = (
                        (mass * sigma) * d + (wxp - wx) + (down_row(wy) - wy)
                        + (jnp.where(lane == 0, ends[j], downs[j]) - wz)
                    )
                    wxp = wx
                    res = NR[f, xp] - applied
                    inside = (row_mask * x_mask(xp)) > 0.0
                    new = jnp.where(inside, keep_part * d + new_part * res, 0.0)
                    if more:
                        NR[f, xp] = res
                        ND[f, xp] = new
                    NY[f, xp] = NY[f, xp] + new

        if n == 1:
            relay(1, copies, QRE, XE, 3)

    @pl.loop(0, N, unroll=4)
    def _(x):
        xp = x + H
        t, g = group_of(xp)
        shift = (251 - 16 * g) & (LANES - 1)
        potential = NY[0, xp]
        last_lane = lane == LANES - 1
        pieces = (
            (NY[0, xp + 1], NY[1, xp], NY[1, xp + 1]),
            (up_row(potential), NY[2, xp], up_row(NY[2, xp])),
            (
                jnp.where(last_lane, roll(PY[0, t], shift, 1), up_lane(potential)),
                NY[3, xp],
                jnp.where(last_lane, roll(PY[3, t], shift, 1), up_lane(NY[3, xp])),
            ),
        )
        for c, (above, own_part, next_part) in enumerate(pieces):
            out[c, x] = ((above - potential) + 0.5 * (own_part + next_part))[OWN]

    finish(copies)

    @pl.loop(0, B, unroll=4)
    def _(xp):
        inside = (row_mask * x_mask(xp)) > 0.0
        for c in range(3):
            E2[c, xp] = jnp.where(inside, E2[c, xp], 0.0)

    assemble(E2, QRE, XE, PE2, 3)
    for colour in range(4):
        turn(colour, E2, PE2, 3 - colour)

    @pl.loop(0, N, unroll=4)
    def _(x):
        for c in range(3):
            out[c, x] = out[c, x] + E2[c, x + H, OWN]


def solution(mesh):
    sizes = tuple(mesh.shape[a] for a in AXES)

    def on_device(right_side, labels, colors, table):
        f32 = jnp.float32
        plain = lambda n: pltpu.VMEM((n, B, B, LANES), f32)
        packed = lambda n: pltpu.VMEM((n, 3, B, LANES), f32)
        across = lambda k: [
            pltpu.VMEM((2, k, N, LANES), f32),
            pltpu.VMEM((2, 2, k, B, LANES), f32),
            pltpu.VMEM((len(RELAYS), k, 8, LANES), f32),
            pltpu.VMEM((2, k, B, LANES), f32),
            pltpu.VMEM((2, k, 2, N, LANES), f32),
        ]
        any_spec = pl.BlockSpec(memory_space=pltpu.HBM)
        return pl.pallas_call(
            functools.partial(kernel, sizes),
            out_shape=jax.ShapeDtypeStruct(right_side.shape, f32),
            in_specs=[any_spec] * 4,
            out_specs=pl.BlockSpec(memory_space=pltpu.VMEM),
            scratch_shapes=[
                pltpu.VMEM((3, N, N, LANES), f32),
                pltpu.VMEM((N, N, LANES), jnp.int32),
                pltpu.VMEM((3, N, N, LANES), jnp.int32),
                pltpu.SMEM((16,), f32),
                plain(7),
                pltpu.VMEM((7, 2, B, LANES), f32),
                pltpu.VMEM((2, 2, 2, B, LANES), f32),
                packed(7),
                pltpu.VMEM((B, B, LANES), f32),
                pltpu.VMEM((3, B, LANES), f32),
                pltpu.VMEM((3, B, LANES), f32),
                pltpu.VMEM((3, B, LANES), f32),
                plain(3),
                packed(3),
                plain(3),
                packed(3),
                pltpu.VMEM((3, 2, B, LANES), f32),
                pltpu.VMEM((2, 1, 2, B, LANES), f32),
                packed(2),
                plain(4),
                plain(4),
                plain(4),
                packed(4),
                packed(4),
                packed(4),
                packed(4),
                *across(2),
                *across(1),
                pltpu.SemaphoreType.DMA((4,)),
                pltpu.SemaphoreType.DMA((2, 2 * len(DIRS) + len(RELAYS))),
                pltpu.SemaphoreType.DMA((2, 2 * len(DIRS) + len(RELAYS))),
            ],
            compiler_params=pltpu.CompilerParams(
                collective_id=0, has_side_effects=True, vmem_limit_bytes=63 * 1024 * 1024
            ),
            cost_estimate=pl.CostEstimate(flops=10**8, bytes_accessed=2 * 10**6, transcendentals=0),
        )(right_side, labels, colors, table)

    in_specs = (P(None, "gx", "gy", "gz"), P("gx", "gy", "gz"), P(None, "gx", "gy", "gz"), P())
    return jax.shard_map(
        on_device, mesh=mesh, in_specs=in_specs, out_specs=P(None, "gx", "gy", "gz"), check_vma=False
    )
```
